32 devices in a mesh: band: 4 (over y, x), tile: 8 (over z, core).
Axes of the slice: x: 2, y: 2, z: 4, core: 2. Of those that a mesh axis runs over, the one named last changes fastest.
Arguments:
- granules: bfloat16 [128, 16, 4096], P('tile', 'band'), may hold values from -6 to 6
- valid_rows: int32 [128, 64], P('tile'), may hold values 0 or 1
- scene_order: int32 [128], P('tile'), may hold values from 0 to 127, each once
- intersections: int32 [128, 4], P('tile'), may hold values from 0 to 7, all different within a row; in each aligned block of 16 rows (0 to 15, 16 to 31, ...) at most 9 rows name the same one
- row_resample: bfloat16 [128, 4, 4096], P('tile'), may hold values from 0 to 1.4, as said below
- col_resample: bfloat16 [128, 4, 4096], P('tile'), may hold values from 0 to 1.4, as said below
- w_in: bfloat16 [16, 256], replicated, may hold values from -1.5 to 1.5
- w_hidden: bfloat16 [2, 256, 256], replicated, may hold values from -0.375 to 0.375
- w_out: bfloat16 [256], replicated, may hold values from -1.5 to 1.5
Outputs:
- composite: float32 [16, 32768], P('band', 'tile')
The draws below stay inside these ranges and needn't reach their ends.
Inputs may be any that keep to these rules, and one draw needn't show every extreme that they name: `intersections`: each scene names 4 different output tiles; the 16 scenes of one device name any one tile at most 9 times, a bound that some block reaches. `scene_order`: each order number appears once. `row_resample`: nonnegative resampling weights. `col_resample`: nonnegative resampling weights.
All inputs are finite; a program needn't handle non-finite values. No bound on the sum of `valid_rows` on one device may be relied on, other than what follows from the above.
Results may differ from the reference program's by a relative error of at most 0.0031.
Values may be sent and summed in bfloat16 or wider, within the bound.
A program may use at most 128 MiB of HBM per device.

```python
import math
import jax
import jax.numpy as jnp
import numpy as np
from jax import lax

BANDS = 16
HID = 256
LAYERS = 2
SIDE = 64
PIX = 4096
SC_DEV = 16
K = 4
HUBER_ITERS = 4
SMOOTH = 2
SCENES = 128
CAP = 9
N_TILE = 8


def resample_matrix(key):
    positions = jnp.arange(SIDE)
    distance = jnp.abs(positions[:, None] - positions[None, :]).astype(jnp.float32)
    on_diagonal = (distance < 0.5).astype(jnp.float32)
    key_diag = jax.random.fold_in(key, 3)
    key_off = jax.random.fold_in(key, 5)
    diag_spread = jax.random.uniform(key_diag, (SCENES, K, SIDE, SIDE), jnp.float32, 0.6, 1.0)
    off_spread = jax.random.uniform(key_off, (SCENES, K, SIDE, SIDE), jnp.float32, 0.5, 1.5)
    dense_scale = 0.5 * SIDE ** (-0.5)
    background = dense_scale * off_spread * jnp.exp(-distance / (0.5 * SIDE))
    matrix = diag_spread * on_diagonal + background
    return matrix.reshape(SCENES, K, SIDE * SIDE).astype(jnp.bfloat16)


def draw_row_resample(key, part):
    return resample_matrix(jax.random.fold_in(key, 11))


def draw_col_resample(key, part):
    return resample_matrix(jax.random.fold_in(key, 23))


def plant(array, rng, least, top_value):
    shape = array.shape
    place = [jax.random.randint(jax.random.fold_in(rng, axis), (), 0, shape[axis]) for axis in range(len(shape))]
    array = array.at[tuple(place)].set(least)
    longest = shape.index(max(shape))
    place[longest] = (place[longest] + 1) % shape[longest]
    return array.at[tuple(place)].set(top_value)


def steps_of(key, dims, shards, least, largest):
    factor_of, own = 1.0, jax.random.fold_in(key, 6)
    for position, parts in shards:
        heights = jnp.exp(jax.random.uniform(jax.random.fold_in(own, position), (parts,), jnp.float32, least / len(shards), largest / len(shards)))
        factor_of = factor_of * jnp.repeat(heights, dims[position] // parts).reshape([-1 if axis == position else 1 for axis in range(len(dims))])
    return factor_of


def assign_block(key, own, number, rows, number_of, top, most, skew):
    sequence = jax.random.permutation(key, number_of)
    crowded, usual = portions_of(number_of, rows * top, most, skew, True), portions_of(number_of, rows * top, most, skew, False)
    places = jnp.arange(number_of)

    def named(tallies, turn):
        used = int((tallies > 0).sum())
        fixed = max(1, used // 4)
        shifted = fixed + (places - fixed + turn * (used - fixed)) % max(1, number_of - fixed)
        return jnp.zeros((number_of,), jnp.int32).at[sequence[jnp.where(places < fixed, places, shifted)]].set(jnp.asarray(tallies, jnp.int32))

    tallies = jnp.where(number % 4 == 0, named(crowded, number // 4), named(usual, number - number // 4 - 1))
    mixed = jax.random.permutation(jax.random.fold_in(own, 3), number_of)
    source_of, sink = mixed[0:number_of // 2 * 2:2], mixed[1:number_of // 2 * 2:2]
    margin = jnp.minimum(tallies[source_of] - 1, most - tallies[sink]) // 2
    margin = jnp.where((source_of == sequence[0]) | (sink == sequence[0]) | (tallies[sink] == 0), 0, jnp.maximum(margin, 0))
    shifted = jax.random.randint(jax.random.fold_in(own, 4), (number_of // 2,), 0, 1 << 20) % (margin + 1)
    tallies = tallies.at[source_of].add(-shifted).at[sink].add(shifted)
    items = jnp.searchsorted(jnp.cumsum(tallies), jnp.arange(rows * top), side="right").astype(jnp.int32)
    table = items.reshape(top, rows).T
    table = table[jax.random.permutation(jax.random.fold_in(own, 1), rows)]
    turn = jax.random.randint(jax.random.fold_in(own, 2), (rows, 1), 0, top)
    return jnp.take_along_axis(table, (jnp.arange(top)[None, :] + turn) % top, axis=1)


def portions_of(count, total, limit, lean, full):
    portions = [(1 << 20) // math.isqrt(standing ** lean) + 1 for standing in range(1, count + 1)]
    largest = limit if full else min(limit, max(-(-total // count), total * portions[0] // sum(portions)))
    least = 1 if total - largest >= count - 1 else 0
    holding, spare = [largest] + [least] * (count - 1), total - largest - least * (count - 1)
    while spare > 0:
        free = [i for i in range(1, count) if holding[i] < largest] or [i for i in range(1, count) if holding[i] < limit]
        whole, left = sum([portions[i] for i in free]), spare
        for i in free:
            extra = min(limit - holding[i], max(1, left * portions[i] // whole), spare)
            holding[i] = holding[i] + extra
            spare = spare - extra
    return np.array(holding)


def centred(rng, shape, scale, reach, pieces=(), kind=jnp.bfloat16):
    values = jax.random.normal(rng, shape, jnp.float32) * scale
    if len(pieces) > 0:
        values = steps_of(rng, shape, pieces, -0.22, 0.18) * values
    return jnp.clip(values, min=-reach, max=reach).astype(kind)


def setup_inputs(seed: int = 0) -> dict:
    arg_keys = jax.random.split(jax.random.key(seed), 10)
    granules = centred(arg_keys[0], (SCENES, BANDS, PIX), 1.0, 6.0, ((0, 8), (1, 4)))
    valid_rows = plant((jax.random.randint(arg_keys[1], (SCENES, SIDE), 0, 4) < 3).astype(jnp.int32), jax.random.fold_in(arg_keys[1], 1), 0, 1)
    scene_order = jax.random.permutation(arg_keys[2], SCENES).astype(jnp.int32)
    intersections_keys = jax.random.split(jax.random.fold_in(arg_keys[3], 1), SCENES // SC_DEV)
    intersections_turns = jax.random.permutation(jax.random.fold_in(arg_keys[3], 3), SCENES // SC_DEV)
    intersections = jax.vmap(lambda own, number: assign_block(jax.random.fold_in(arg_keys[3], 2), own, number, SC_DEV, N_TILE, K, CAP, 2))(intersections_keys, intersections_turns).reshape((SCENES, K))
    row_resample = draw_row_resample(jax.random.fold_in(arg_keys[9], 71), 0)
    col_resample = draw_col_resample(jax.random.fold_in(arg_keys[9], 71), 0)
    w_in = centred(arg_keys[6], (BANDS, HID), BANDS ** -0.5, 1.5)
    w_hidden = centred(arg_keys[7], (LAYERS, HID, HID), HID ** -0.5, 0.375)
    w_out = centred(arg_keys[8], (HID,), 0.25, 1.5)
    return dict(granules=granules, valid_rows=valid_rows, scene_order=scene_order, intersections=intersections, row_resample=row_resample, col_resample=col_resample, w_in=w_in, w_hidden=w_hidden, w_out=w_out)


prior_weight = 0.25
huber_delta = 0.5
edge_scale = 1.0
smooth_rate = 0.2


def cloud_weight(pixels, valid_pix, recency, w_in, w_hidden, w_out):
    hidden = jax.nn.silu(jnp.dot(pixels.T, w_in, preferred_element_type=jnp.float32)).astype(jnp.bfloat16)
    for repeat in range(LAYERS):
        hidden = jax.nn.silu(jnp.dot(hidden, w_hidden[repeat], preferred_element_type=jnp.float32)).astype(jnp.bfloat16)
    logits = jnp.dot(hidden, w_out, preferred_element_type=jnp.float32)
    return (jax.nn.sigmoid(-logits) * valid_pix * recency).astype(jnp.bfloat16)


def reproject(planes, rows_matrix, cols_matrix):
    half_done = jnp.einsum('ncil,njl->ncij', planes.astype(jnp.float32), cols_matrix.astype(jnp.float32)).astype(jnp.bfloat16)
    return jnp.einsum('nij,ncjl->ncil', rows_matrix.astype(jnp.float32), half_done.astype(jnp.float32)).astype(jnp.bfloat16)


def huber_merge(observed, weights):
    values = observed.astype(jnp.float32)
    plain = weights.astype(jnp.float32)[:, None, :]
    estimate = jnp.sum(plain * values, 0) / (jnp.sum(plain, 0) + prior_weight)
    for repeat in range(HUBER_ITERS):
        residual = values - estimate[None]
        huber_w = plain * huber_delta / jnp.maximum(jnp.abs(residual), huber_delta)
        estimate = jnp.sum(huber_w * values, 0) / (jnp.sum(huber_w, 0) + prior_weight)
    return estimate


def smooth_step(extended, first_col, total_cols):
    positions = first_col + jnp.arange(extended.shape[2] - 1)
    inside = ((positions >= 0) & (positions + 1 < total_cols)).astype(jnp.float32)
    across = extended[:, :, 1:] - extended[:, :, :-1]
    sideways = across / (1.0 + (across / edge_scale) ** 2) * inside
    centre = extended[:, :, 1:-1]
    upward_diff = centre[:, 1:, :] - centre[:, :-1, :]
    upward = upward_diff / (1.0 + (upward_diff / edge_scale) ** 2)
    zeros_row = jnp.zeros_like(upward[:, :1, :])
    vertical = jnp.concatenate([upward, zeros_row], 1) - jnp.concatenate([zeros_row, upward], 1)
    return centre + smooth_rate * (sideways[:, :, 1:] - sideways[:, :, :-1] + vertical)


def reference(granules, valid_rows, scene_order, intersections, row_resample, col_resample, w_in, w_hidden, w_out):
    recency = jnp.exp(1.4 * scene_order.astype(jnp.float32) / SCENES - 0.7)

    def one_scene(scene):
        valid_pix = jnp.repeat(valid_rows[scene].astype(jnp.float32), SIDE)
        return cloud_weight(granules[scene], valid_pix, recency[scene], w_in, w_hidden, w_out)

    weights = lax.map(one_scene, jnp.arange(SCENES).astype(jnp.int32))
    planes = jnp.concatenate([granules, weights[:, None, :]], 1)
    flat_dest = intersections.reshape(SCENES * K)
    entry_count = SCENES * K
    slot_count = N_TILE * CAP

    def one_owner(owner):
        sort_key = jnp.where(flat_dest == owner, jnp.arange(entry_count).astype(jnp.int32), entry_count).astype(jnp.int32)
        chosen = jnp.argsort(sort_key)[:slot_count].astype(jnp.int32)
        present = (sort_key[chosen] < entry_count).astype(jnp.bfloat16)
        scene_of = chosen // K
        which_k = chosen % K
        taken = planes[scene_of].reshape(slot_count, BANDS + 1, SIDE, SIDE)
        rows_taken = row_resample[scene_of, which_k].reshape(slot_count, SIDE, SIDE)
        cols_taken = col_resample[scene_of, which_k].reshape(slot_count, SIDE, SIDE)
        moved = reproject(taken, rows_taken, cols_taken)
        moved = moved.reshape(slot_count, BANDS + 1, PIX)
        return huber_merge(moved[:, :BANDS], moved[:, BANDS] * present[:, None])

    estimates = lax.map(one_owner, jnp.arange(N_TILE).astype(jnp.int32))
    field = estimates.reshape(N_TILE, BANDS, SIDE, SIDE).transpose(1, 2, 0, 3).reshape(BANDS, SIDE, N_TILE * SIDE)
    for repeat in range(SMOOTH):
        extended = jnp.pad(field, ((0, 0), (0, 0), (1, 1)))
        field = smooth_step(extended, -1, N_TILE * SIDE)
    return field.reshape(BANDS, SIDE, N_TILE, SIDE).transpose(0, 2, 1, 3).reshape(BANDS, N_TILE * PIX)
```

```python
import functools

import jax
import jax.numpy as jnp
import numpy as np
from jax import lax
from jax.experimental import pallas as pl
from jax.experimental.pallas import tpu as pltpu
from jax.sharding import PartitionSpec as P

HUBER_ITERS = 4
SMOOTH = 2
prior_weight = 0.25
huber_delta = 0.5
edge_scale = 1.0
smooth_rate = 0.2
BF = jnp.bfloat16
F32 = jnp.float32


def mlp_kernel(x_ref, scale_ref, w_in_ref, w_hid_ref, w_out_ref, out_ref):
    bands = [x_ref[b, 0] for b in range(x_ref.shape[0])]
    x = jnp.concatenate(bands, axis=0)

    def silu(t):
        return (t + t * jnp.tanh(t)).astype(BF)

    hidden = silu(jnp.dot(w_in_ref[...], x, preferred_element_type=F32))
    for layer in range(w_hid_ref.shape[0]):
        hidden = silu(jnp.dot(w_hid_ref[layer], hidden, preferred_element_type=F32))
    logits = jnp.dot(w_out_ref[...], hidden, preferred_element_type=F32)
    row = jax.nn.sigmoid(-logits[0:1])
    pieces = [row[:, i * 128 : (i + 1) * 128] for i in range(row.shape[1] // 128)]
    out_ref[0] = (jnp.concatenate(pieces, axis=0) * scale_ref[0]).astype(BF)


def cloud_weights(x, scale, w_in, w_hidden, w_out):
    groups, scenes, part, width = x.shape
    hid = w_in.shape[1]
    layers = w_hidden.shape[0]
    half = jnp.asarray(0.5, BF)
    w_in_t = (w_in * half).T
    w_hid_t = jnp.swapaxes(w_hidden * half, 1, 2)
    w_out_t = jnp.broadcast_to(w_out[None, :], (16, hid))
    lines = width // 128
    return pl.pallas_call(
        mlp_kernel,
        grid=(scenes,),
        in_specs=[
            pl.BlockSpec((groups, 1, part, width), lambda s: (0, s, 0, 0)),
            pl.BlockSpec((1, lines, 128), lambda s: (s, 0, 0)),
            pl.BlockSpec((hid, groups * part), lambda s: (0, 0)),
            pl.BlockSpec((layers, hid, hid), lambda s: (0, 0, 0)),
            pl.BlockSpec((16, hid), lambda s: (0, 0)),
        ],
        out_specs=pl.BlockSpec((1, lines, 128), lambda s: (s, 0, 0)),
        out_shape=jax.ShapeDtypeStruct((scenes, lines, 128), BF),
        compiler_params=pltpu.CompilerParams(vmem_limit_bytes=32 * 1024 * 1024),
        cost_estimate=pl.CostEstimate(
            flops=scenes * width * 2 * hid * (16 + layers * hid),
            bytes_accessed=4 * 1024 * 1024,
            transcendentals=scenes * width * hid * 3,
        ),
    )(x, scale, w_in_t, w_hid_t, w_out_t)


def merge_kernel(
    cap, scene_ref, present_ref, x_ref, w_ref, m_ref, q_ref, u_ref, v_ref, out_ref, y_ref, wt_ref
):
    source = pl.program_id(0)
    lane = lax.broadcasted_iota(jnp.int32, (32, 128), 1)
    low = lane < 64
    quarters = range(m_ref.shape[0])
    for r in range(cap):
        slot = source * cap + r
        scene = scene_ref[slot]
        planes = x_ref[scene]
        weight = jnp.concatenate([w_ref[0, b, scene] for b in quarters], axis=0)
        rows = jnp.concatenate([m_ref[b, r, 0:8] for b in quarters], axis=0)
        cols = jnp.concatenate([m_ref[b, r, 8:16] for b in quarters], axis=0).astype(F32)
        turned = pltpu.roll(cols, 64, 1)
        zero = jnp.zeros((32, 128), F32)
        first = jnp.concatenate([jnp.where(low, cols, zero), jnp.where(low, turned, zero)], 0)
        second = jnp.concatenate([jnp.where(low, zero, turned), jnp.where(low, zero, cols)], 0)
        first, second = first.astype(BF), second.astype(BF)
        blank = jnp.zeros((64, 128), BF)
        right = jnp.concatenate(
            [
                jnp.concatenate([first, blank], 1),
                jnp.concatenate([blank, first], 1),
                jnp.concatenate([second, blank], 1),
                jnp.concatenate([blank, second], 1),
            ],
            0,
        )
        left = jnp.concatenate(
            [
                jnp.concatenate([planes[0], planes[1]], 1),
                jnp.concatenate([planes[2], planes[3]], 1),
                jnp.concatenate([weight, weight], 1),
            ],
            0,
        )
        half = lax.dot_general(
            left, right, (((1,), (1,)), ((), ())), preferred_element_type=F32
        ).astype(BF)
        stacked = jnp.concatenate(
            [
                jnp.concatenate([half[p * 32 : p * 32 + 32, 0:128] for p in range(3)], 1),
                jnp.concatenate([half[p * 32 : p * 32 + 32, 128:256] for p in range(3)], 1),
            ],
            0,
        )
        spread = jnp.dot(rows, q_ref[...], preferred_element_type=F32).astype(BF)
        row_matrix = jnp.concatenate([spread[:, 0:64], spread[:, 128:192]], 0)
        moved = jnp.dot(row_matrix, stacked, preferred_element_type=F32)
        present = present_ref[slot].astype(F32)
        y_ref[slot] = moved[:, 0:256].astype(BF)
        wt_ref[slot] = (moved[:, 256:384] * present).astype(BF)

    @pl.when(source == pl.num_programs(0) - 1)
    def _():
        slots = y_ref.shape[0]
        chunk = 16

        def merge_rows(i, carry):
            here = pl.ds(pl.multiple_of(i * chunk, chunk), chunk)

            def load(n):
                y = y_ref[n, here, :].astype(F32)
                w = wt_ref[n, here, :].astype(F32)
                return y, jnp.concatenate([w, w], 1)

            def plain(n, sums):
                y, w = load(n)
                return sums[0] + w * y, sums[1] + w

            def robust(estimate, n, sums):
                y, w = load(n)
                size = jnp.maximum(jnp.abs(y - estimate), huber_delta)
                h = w * (huber_delta * pl.reciprocal(size, approx=True))
                return sums[0] + h * y, sums[1] + h

            empty = (jnp.zeros((chunk, 256), F32), jnp.zeros((chunk, 256), F32))
            top, bottom = lax.fori_loop(0, slots, plain, empty, unroll=4)
            estimate = top / (bottom + prior_weight)
            for _ in range(HUBER_ITERS):
                top, bottom = lax.fori_loop(
                    0, slots, functools.partial(robust, estimate), empty, unroll=4
                )
                estimate = top / (bottom + prior_weight)
            out_ref[here, :] = estimate
            return carry

        lax.fori_loop(0, 64 // chunk, merge_rows, 0)
        exact = lax.Precision.HIGHEST
        ordered = jnp.dot(u_ref[...], out_ref[...], precision=exact, preferred_element_type=F32)
        out_ref[:, 0:128] = jnp.dot(
            ordered[:, 0:128], v_ref[...], precision=exact, preferred_element_type=F32
        )
        out_ref[:, 128:256] = jnp.dot(
            ordered[:, 128:256], v_ref[...], precision=exact, preferred_element_type=F32
        )


def order_matrices():
    q = np.zeros((128, 256), np.float32)
    u = np.zeros((64, 64), np.float32)
    v = np.zeros((128, 128), np.float32)
    for n in range(64):
        place = (n % 2) * 32 + n // 2
        q[n, place] = 1
        q[64 + n, 128 + place] = 1
        u[n, place] = 1
        v[place, n] = 1
        v[64 + place, 64 + n] = 1
    return jnp.asarray(q, BF), jnp.asarray(u), jnp.asarray(v)


def merge(scene_of, present, planes, weights, matrices, cap):
    sources, quarters, scenes, lines, _ = weights.shape
    slots = sources * cap
    q, u, v = order_matrices()
    return pl.pallas_call(
        functools.partial(merge_kernel, cap),
        grid_spec=pltpu.PrefetchScalarGridSpec(
            num_scalar_prefetch=2,
            grid=(sources,),
            in_specs=[
                pl.BlockSpec((scenes, 4, 32, 128), lambda d, *_: (d, 0, 0, 0)),
                pl.BlockSpec((1, quarters, scenes, lines, 128), lambda d, *_: (d, 0, 0, 0, 0)),
                pl.BlockSpec((quarters, cap, 16, 128), lambda d, *_: (0, d, 0, 0)),
                pl.BlockSpec((128, 256), lambda d, *_: (0, 0)),
                pl.BlockSpec((64, 64), lambda d, *_: (0, 0)),
                pl.BlockSpec((128, 128), lambda d, *_: (0, 0)),
            ],
            out_specs=pl.BlockSpec((64, 256), lambda d, *_: (0, 0)),
            scratch_shapes=[
                pltpu.VMEM((slots, 64, 256), BF),
                pltpu.VMEM((slots, 64, 128), BF),
            ],
        ),
        out_shape=jax.ShapeDtypeStruct((64, 256), F32),
        compiler_params=pltpu.CompilerParams(vmem_limit_bytes=40 * 1024 * 1024),
        cost_estimate=pl.CostEstimate(
            flops=slots * 40_000_000, bytes_accessed=8 * 1024 * 1024, transcendentals=slots * 65536
        ),
    )(scene_of, present, planes, weights, matrices, q, u, v)


def smooth_step(extended, first_col, total_cols):
    positions = first_col + jnp.arange(extended.shape[2] - 1)
    inside = ((positions >= 0) & (positions + 1 < total_cols)).astype(F32)
    across = extended[:, :, 1:] - extended[:, :, :-1]
    sideways = across / (1.0 + (across / edge_scale) ** 2) * inside
    centre = extended[:, :, 1:-1]
    upward_diff = centre[:, 1:, :] - centre[:, :-1, :]
    upward = upward_diff / (1.0 + (upward_diff / edge_scale) ** 2)
    zeros_row = jnp.zeros_like(upward[:, :1, :])
    vertical = jnp.concatenate([upward, zeros_row], 1) - jnp.concatenate([zeros_row, upward], 1)
    return centre + smooth_rate * (sideways[:, :, 1:] - sideways[:, :, :-1] + vertical)


def per_device(
    granules,
    valid_rows,
    scene_order,
    intersections,
    row_resample,
    col_resample,
    w_in,
    w_hidden,
    w_out,
):
    scenes, group_bands, pixel_count = granules.shape
    side_cells = valid_rows.shape[1]
    top = intersections.shape[1]
    tile_count = lax.axis_size("tile")
    band_count = lax.axis_size("band")
    band = lax.axis_index("band")
    tile = lax.axis_index("tile")
    entry_count = scenes * top
    cap = (entry_count + tile_count - 1) // tile_count + 1
    part = pixel_count // band_count
    row_count = side_cells // band_count

    laid = granules.reshape(scenes, group_bands, pixel_count // 128, 128)
    planes = lax.all_gather(laid, "tile", axis=0, tiled=True)

    quarters = jnp.stack([granules[:, :, b * part : (b + 1) * part] for b in range(band_count)])
    by_rows = lax.all_to_all(quarters, "band", split_axis=0, concat_axis=0, tiled=True)
    recency = jnp.exp(1.4 * scene_order.astype(F32) / (scenes * tile_count) - 0.7)
    valid_here = lax.dynamic_slice_in_dim(valid_rows, band * row_count, row_count, 1).astype(F32)
    scale = valid_here * recency[:, None]
    scale = jnp.broadcast_to(scale[:, :, None], (scenes, row_count, side_cells))
    scale = scale.reshape(scenes, part // 128, 128)
    own_weights = cloud_weights(by_rows, scale, w_in, w_hidden, w_out)
    weights = lax.all_gather(own_weights, ("tile", "band"), axis=0, tiled=False)
    weights = weights.reshape((tile_count, band_count) + own_weights.shape)

    flat_dest = intersections.reshape(entry_count)
    is_dest = flat_dest[None, :] == jnp.arange(tile_count, dtype=jnp.int32)[:, None]
    rank = jnp.cumsum(is_dest.astype(jnp.int32), 1) - 1
    pick = is_dest[:, None, :] & (rank[:, None, :] == jnp.arange(cap)[None, :, None])
    pick = pick.reshape(tile_count * cap, entry_count).astype(BF)
    both = jnp.concatenate(
        [
            lax.dynamic_slice_in_dim(m, band * part, part, 2).reshape(entry_count, part)
            for m in (row_resample, col_resample)
        ],
        1,
    )
    sent = jnp.dot(pick, both, preferred_element_type=F32).astype(BF)
    sent = sent.reshape(tile_count * cap, 2 * part // 128, 128)
    got = lax.all_to_all(sent, "tile", split_axis=0, concat_axis=0, tiled=True)
    matrices = lax.all_gather(got, "band", axis=0, tiled=False)

    everywhere = lax.all_gather(intersections, "tile", axis=0, tiled=False)
    named = jnp.any(everywhere == tile, axis=2)
    order = jnp.cumsum(named.astype(jnp.int32), 1) - 1
    chosen = named[:, None, :] & (order[:, None, :] == jnp.arange(cap)[None, :, None])
    scene_of = jnp.sum(jnp.where(chosen, jnp.arange(scenes)[None, None, :], 0), 2)
    scene_of = scene_of.reshape(-1).astype(jnp.int32)
    present = jnp.any(chosen, 2).reshape(-1).astype(jnp.int32)

    estimate = merge(scene_of, present, planes, weights, matrices, cap)
    field = estimate.reshape(side_cells, group_bands, side_cells).transpose(1, 0, 2)

    forward = [(i, i + 1) for i in range(tile_count - 1)]
    backward = [(i + 1, i) for i in range(tile_count - 1)]
    low = lax.ppermute(field[:, :, side_cells - SMOOTH :], "tile", forward)
    high = lax.ppermute(field[:, :, :SMOOTH], "tile", backward)
    field = jnp.concatenate([low, field, high], 2)
    for step in range(SMOOTH):
        first_col = tile * side_cells - SMOOTH + step
        field = smooth_step(field, first_col, tile_count * side_cells)
    return field.reshape(group_bands, pixel_count)


def solution(mesh):
    return jax.shard_map(
        per_device,
        mesh=mesh,
        in_specs=(
            P("tile", "band", None),
            P("tile", None),
            P("tile"),
            P("tile", None),
            P("tile", None, None),
            P("tile", None, None),
            P(),
            P(),
            P(),
        ),
        out_specs=P("band", "tile"),
        check_vma=False,
    )
```

```python
import functools

import jax
import jax.numpy as jnp
import numpy as np
from jax import lax
from jax.experimental import pallas as pl
from jax.experimental.pallas import tpu as pltpu
from jax.sharding import PartitionSpec as P

HUBER_ITERS = 4
SMOOTH = 2
prior_weight = 0.25
huber_delta = 0.5
edge_scale = 1.0
smooth_rate = 0.2
BF = jnp.bfloat16
F32 = jnp.float32


MESH = pl.DeviceIdType.MESH


def exchange_kernel(
    segment,
    quarters_ref,
    laid_ref,
    sent_ref,
    meta_ref,
    scale_ref,
    w_in_ref,
    w_hid_ref,
    w_out_ref,
    planes_ref,
    weights_ref,
    matrices_ref,
    codes_ref,
    x_ref,
    own_ref,
    local_sems,
    x_send,
    x_recv,
    right_send,
    left_send,
    plane_recv,
    mat_send,
    mat_recv,
    code_send,
    code_recv,
    weight_send,
    weight_recv,
    mat_band_send,
    mat_band_recv,
    weight_band_send,
    weight_band_recv,
):
    tiles = planes_ref.shape[0]
    bands = quarters_ref.shape[0]
    scenes = laid_ref.shape[0]
    cap = sent_ref.shape[0] // tiles
    tile = lax.axis_index("tile")
    band = lax.axis_index("band")

    def tile_peer(k):
        return lax.rem(tile + k, tiles)

    def tile_source(k):
        return lax.rem(tile + tiles - k, tiles)

    def band_peer(k):
        return lax.rem(band + k, bands)

    def for_tiles(first, body):
        def step(k, carry):
            body(k)
            return carry

        lax.fori_loop(first, tiles, step, 0)

    barrier = pltpu.get_barrier_semaphore()
    for_tiles(
        1,
        lambda k: pl.semaphore_signal(
            barrier, inc=1, device_id={"tile": tile_peer(k)}, device_id_type=MESH
        ),
    )
    for k in range(1, bands):
        pl.semaphore_signal(barrier, inc=1, device_id={"band": band_peer(k)}, device_id_type=MESH)
    pl.semaphore_wait(barrier, tiles - 1 + bands - 1)

    def remote(src, dst, send, recv, where):
        return pltpu.make_async_remote_copy(
            src_ref=src,
            dst_ref=dst,
            send_sem=send,
            recv_sem=recv,
            device_id=where,
            device_id_type=MESH,
        )

    def x_copy(peer, source):
        return remote(
            quarters_ref.at[peer], x_ref.at[source], x_send.at[peer], x_recv.at[source],
            {"band": peer},
        )

    def plane_copy(shard, target, sems):
        return remote(
            planes_ref.at[shard], planes_ref.at[shard], sems.at[shard], plane_recv.at[shard],
            {"tile": target},
        )

    def own_plane_copy(target, sems):
        return remote(
            laid_ref, planes_ref.at[tile], sems.at[tile], plane_recv.at[tile], {"tile": target}
        )

    def mat_copy(peer, source):
        return remote(
            sent_ref.at[pl.ds(peer * cap, cap)], matrices_ref.at[band, source],
            mat_send.at[peer], mat_recv.at[source], {"tile": peer},
        )

    def code_copy(peer, source):
        return remote(
            meta_ref.at[peer], codes_ref.at[source], code_send.at[peer], code_recv.at[source],
            {"tile": peer},
        )

    def weight_copy(peer, source):
        return remote(
            own_ref, weights_ref.at[band, source], weight_send.at[peer], weight_recv.at[source],
            {"tile": peer},
        )

    def mat_band_copy(source, peer, owner):
        return remote(
            matrices_ref.at[owner, source], matrices_ref.at[owner, source],
            mat_band_send.at[peer], mat_band_recv.at[owner], {"band": peer},
        )

    def weight_band_copy(source, peer, owner):
        return remote(
            weights_ref.at[owner, source], weights_ref.at[owner, source],
            weight_band_send.at[peer], weight_band_recv.at[owner], {"band": peer},
        )

    for k in range(1, bands):
        x_copy(band_peer(k), band).start()
    x_local = pltpu.make_async_copy(quarters_ref.at[band], x_ref.at[band], local_sems.at[0])
    x_local.start()

    @pl.when(tile < tiles - 1)
    def _():
        own_plane_copy(tile + 1, right_send).start()

    @pl.when(tile > 0)
    def _():
        own_plane_copy(tile - 1, left_send).start()

    def first_sends(k):
        mat_copy(tile_peer(k), tile).start()
        code_copy(tile_peer(k), tile).start()

    for_tiles(1, first_sends)
    plane_local = pltpu.make_async_copy(laid_ref, planes_ref.at[tile], local_sems.at[1])
    plane_local.start()
    mat_local = pltpu.make_async_copy(
        sent_ref.at[pl.ds(tile * cap, cap)], matrices_ref.at[band, tile], local_sems.at[2]
    )
    mat_local.start()
    code_local = pltpu.make_async_copy(meta_ref.at[tile], codes_ref.at[tile], local_sems.at[3])
    code_local.start()

    def forward(s):
        left, right = tile - s, tile + s

        @pl.when(left >= 0)
        def _():
            plane_copy(left, tile, right_send).wait_recv()

            @pl.when(tile < tiles - 1)
            def _():
                plane_copy(left, tile + 1, right_send).start()

        @pl.when(right < tiles)
        def _():
            plane_copy(right, tile, left_send).wait_recv()

            @pl.when(tile > 0)
            def _():
                plane_copy(right, tile - 1, left_send).start()

    def network(scene, carry):
        def silu(t):
            return (t + t * jnp.tanh(t)).astype(BF)

        x = jnp.concatenate([x_ref[b, scene] for b in range(bands)], axis=0)
        hidden = silu(jnp.dot(w_in_ref[...], x, preferred_element_type=F32))
        for layer in range(w_hid_ref.shape[0]):
            hidden = silu(jnp.dot(w_hid_ref[layer], hidden, preferred_element_type=F32))
        logits = jnp.dot(w_out_ref[...], hidden, preferred_element_type=F32)
        row = jax.nn.sigmoid(-logits[0:1])
        pieces = [row[:, i * 128 : (i + 1) * 128] for i in range(row.shape[1] // 128)]
        own_ref[scene] = (jnp.concatenate(pieces, axis=0) * scale_ref[scene]).astype(BF)
        return carry

    def share_matrices():
        mat_local.wait()
        for k in range(1, bands):
            mat_band_copy(tile, band_peer(k), band).start()

        def share(k):
            source = tile_source(k)
            mat_copy(tile, source).wait_recv()
            for j in range(1, bands):
                mat_band_copy(source, band_peer(j), band).start()

        for_tiles(1, share)

    for k in range(1, bands):
        source = lax.rem(band + bands - k, bands)
        x_copy(source, source).wait_recv()
    x_local.wait()
    steps = 1
    for start in range(0, scenes, segment):
        lax.fori_loop(start, start + segment, network, 0)
        if steps < tiles:
            forward(steps)
            steps += 1
        if start == 2 * segment:
            share_matrices()

    weight_local = pltpu.make_async_copy(own_ref, weights_ref.at[band, tile], local_sems.at[4])
    weight_local.start()
    for_tiles(1, lambda k: weight_copy(tile_peer(k), tile).start())
    weight_local.wait()
    for k in range(1, bands):
        weight_band_copy(tile, band_peer(k), band).start()

    def share_weights(k):
        source = tile_source(k)
        weight_copy(tile, source).wait_recv()
        for j in range(1, bands):
            weight_band_copy(source, band_peer(j), band).start()

    if steps < tiles:
        forward(steps)
        steps += 1
    for_tiles(1, share_weights)
    for_tiles(steps, forward)

    plane_local.wait()
    code_local.wait()

    def finish(k):
        code_copy(tile, tile_source(k)).wait_recv()
        code_copy(tile_peer(k), tile).wait_send()
        mat_copy(tile_peer(k), tile).wait_send()
        weight_copy(tile_peer(k), tile).wait_send()

    for_tiles(1, finish)

    def finish_planes(shard):
        @pl.when((shard <= tile) & (tile < tiles - 1))
        def _():
            plane_copy(shard, tile, right_send).wait_send()

        @pl.when((shard >= tile) & (tile > 0))
        def _():
            plane_copy(shard, tile, left_send).wait_send()

    for_tiles(0, finish_planes)
    for k in range(1, bands):
        peer = band_peer(k)
        x_copy(peer, band).wait_send()
        for ref, send, recv in (
            (matrices_ref, mat_band_send, mat_band_recv),
            (weights_ref, weight_band_send, weight_band_recv),
        ):
            whole = remote(ref.at[peer], ref.at[peer], send.at[peer], recv.at[peer], {"band": peer})
            whole.wait_send()
            whole.wait_recv()


def exchange(quarters, laid, sent, meta, scale, w_in, w_hidden, w_out):
    bands, scenes, part, width = quarters.shape
    tiles = meta.shape[0]
    cap = sent.shape[0] // tiles
    hid = w_in.shape[1]
    layers = w_hidden.shape[0]
    half = jnp.asarray(0.5, BF)
    w_in_t = (w_in * half).T
    w_hid_t = jnp.swapaxes(w_hidden * half, 1, 2)
    w_out_t = jnp.broadcast_to(w_out[None, :], (16, hid))
    lines = width // 128
    anywhere = pl.BlockSpec(memory_space=pl.ANY)
    vmem = pl.BlockSpec(memory_space=pltpu.VMEM)
    dma = pltpu.SemaphoreType.DMA
    return pl.pallas_call(
        functools.partial(exchange_kernel, max(1, scenes // 4)),
        in_specs=[anywhere] * 4 + [vmem] * 4,
        out_specs=[anywhere] * 4,
        out_shape=[
            jax.ShapeDtypeStruct((tiles,) + laid.shape, BF),
            jax.ShapeDtypeStruct((bands, tiles, scenes, lines, 128), BF),
            jax.ShapeDtypeStruct((bands, tiles, cap) + sent.shape[1:], BF),
            jax.ShapeDtypeStruct(meta.shape, jnp.int32),
        ],
        scratch_shapes=[
            pltpu.VMEM(quarters.shape, BF),
            pltpu.VMEM((scenes, lines, 128), BF),
            dma((5,)),
            dma((bands,)),
            dma((bands,)),
        ]
        + [dma((tiles,))] * 9
        + [dma((bands,))] * 4,
        compiler_params=pltpu.CompilerParams(
            collective_id=0, has_side_effects=True, vmem_limit_bytes=32 * 1024 * 1024
        ),
    )(quarters, laid, sent, meta, scale, w_in_t, w_hid_t, w_out_t)


def merge_kernel(
    cap, code_ref, x_ref, w_ref, m_ref, q_ref, u_ref, v_ref, out_ref, y_ref, wt_ref
):
    source = pl.program_id(0)
    lane = lax.broadcasted_iota(jnp.int32, (32, 128), 1)
    low = lane < 64
    quarters = range(m_ref.shape[0])
    for r in range(cap):
        slot = source * cap + r
        code = code_ref[slot]
        scene = jnp.maximum(code, 0)
        planes = x_ref[0, scene]
        weight = jnp.concatenate([w_ref[b, 0, scene] for b in quarters], axis=0)
        rows = jnp.concatenate([m_ref[b, 0, r, 0:8] for b in quarters], axis=0)
        cols = jnp.concatenate([m_ref[b, 0, r, 8:16] for b in quarters], axis=0).astype(F32)
        turned = pltpu.roll(cols, 64, 1)
        zero = jnp.zeros((32, 128), F32)
        first = jnp.concatenate([jnp.where(low, cols, zero), jnp.where(low, turned, zero)], 0)
        second = jnp.concatenate([jnp.where(low, zero, turned), jnp.where(low, zero, cols)], 0)
        first, second = first.astype(BF), second.astype(BF)
        blank = jnp.zeros((64, 128), BF)
        right = jnp.concatenate(
            [
                jnp.concatenate([first, blank], 1),
                jnp.concatenate([blank, first], 1),
                jnp.concatenate([second, blank], 1),
                jnp.concatenate([blank, second], 1),
            ],
            0,
        )
        left = jnp.concatenate(
            [
                jnp.concatenate([planes[0], planes[1]], 1),
                jnp.concatenate([planes[2], planes[3]], 1),
                jnp.concatenate([weight, weight], 1),
            ],
            0,
        )
        half = lax.dot_general(
            left, right, (((1,), (1,)), ((), ())), preferred_element_type=F32
        ).astype(BF)
        stacked = jnp.concatenate(
            [
                jnp.concatenate([half[p * 32 : p * 32 + 32, 0:128] for p in range(3)], 1),
                jnp.concatenate([half[p * 32 : p * 32 + 32, 128:256] for p in range(3)], 1),
            ],
            0,
        )
        spread = jnp.dot(rows, q_ref[...], preferred_element_type=F32).astype(BF)
        row_matrix = jnp.concatenate([spread[:, 0:64], spread[:, 128:192]], 0)
        moved = jnp.dot(row_matrix, stacked, preferred_element_type=F32)
        present = jnp.where(code >= 0, 1.0, 0.0)
        y_ref[slot] = moved[:, 0:256].astype(BF)
        wt_ref[slot] = (moved[:, 256:384] * present).astype(BF)

    @pl.when(source == pl.num_programs(0) - 1)
    def _():
        slots = y_ref.shape[0]
        chunk = 16

        def merge_rows(i, carry):
            here = pl.ds(pl.multiple_of(i * chunk, chunk), chunk)

            def load(n):
                y = y_ref[n, here, :].astype(F32)
                w = wt_ref[n, here, :].astype(F32)
                return y, jnp.concatenate([w, w], 1)

            def plain(n, sums):
                y, w = load(n)
                return sums[0] + w * y, sums[1] + w

            def robust(estimate, n, sums):
                y, w = load(n)
                size = jnp.maximum(jnp.abs(y - estimate), huber_delta)
                h = w * (huber_delta * pl.reciprocal(size, approx=True))
                return sums[0] + h * y, sums[1] + h

            empty = (jnp.zeros((chunk, 256), F32), jnp.zeros((chunk, 256), F32))
            top, bottom = lax.fori_loop(0, slots, plain, empty, unroll=4)
            estimate = top / (bottom + prior_weight)
            for _ in range(HUBER_ITERS):
                top, bottom = lax.fori_loop(
                    0, slots, functools.partial(robust, estimate), empty, unroll=4
                )
                estimate = top / (bottom + prior_weight)
            out_ref[here, :] = estimate
            return carry

        lax.fori_loop(0, 64 // chunk, merge_rows, 0)
        exact = lax.Precision.HIGHEST
        ordered = jnp.dot(u_ref[...], out_ref[...], precision=exact, preferred_element_type=F32)
        out_ref[:, 0:128] = jnp.dot(
            ordered[:, 0:128], v_ref[...], precision=exact, preferred_element_type=F32
        )
        out_ref[:, 128:256] = jnp.dot(
            ordered[:, 128:256], v_ref[...], precision=exact, preferred_element_type=F32
        )


def order_matrices():
    q = np.zeros((128, 256), np.float32)
    u = np.zeros((64, 64), np.float32)
    v = np.zeros((128, 128), np.float32)
    for n in range(64):
        place = (n % 2) * 32 + n // 2
        q[n, place] = 1
        q[64 + n, 128 + place] = 1
        u[n, place] = 1
        v[place, n] = 1
        v[64 + place, 64 + n] = 1
    return jnp.asarray(q, BF), jnp.asarray(u), jnp.asarray(v)


def merge(codes, planes, weights, matrices):
    quarters, sources, scenes, lines, _ = weights.shape
    cap = matrices.shape[2]
    slots = sources * cap
    q, u, v = order_matrices()
    return pl.pallas_call(
        functools.partial(merge_kernel, cap),
        grid_spec=pltpu.PrefetchScalarGridSpec(
            num_scalar_prefetch=1,
            grid=(sources,),
            in_specs=[
                pl.BlockSpec((1, scenes, 4, 32, 128), lambda d, *_: (d, 0, 0, 0, 0)),
                pl.BlockSpec((quarters, 1, scenes, lines, 128), lambda d, *_: (0, d, 0, 0, 0)),
                pl.BlockSpec((quarters, 1, cap, 16, 128), lambda d, *_: (0, d, 0, 0, 0)),
                pl.BlockSpec((128, 256), lambda d, *_: (0, 0)),
                pl.BlockSpec((64, 64), lambda d, *_: (0, 0)),
                pl.BlockSpec((128, 128), lambda d, *_: (0, 0)),
            ],
            out_specs=pl.BlockSpec((64, 256), lambda d, *_: (0, 0)),
            scratch_shapes=[
                pltpu.VMEM((slots, 64, 256), BF),
                pltpu.VMEM((slots, 64, 128), BF),
            ],
        ),
        out_shape=jax.ShapeDtypeStruct((64, 256), F32),
        compiler_params=pltpu.CompilerParams(vmem_limit_bytes=40 * 1024 * 1024),
        cost_estimate=pl.CostEstimate(
            flops=slots * 40_000_000, bytes_accessed=8 * 1024 * 1024, transcendentals=slots * 65536
        ),
    )(codes, planes, weights, matrices, q, u, v)


def smooth_step(extended, first_col, total_cols):
    positions = first_col + jnp.arange(extended.shape[2] - 1)
    inside = ((positions >= 0) & (positions + 1 < total_cols)).astype(F32)
    across = extended[:, :, 1:] - extended[:, :, :-1]
    sideways = across / (1.0 + (across / edge_scale) ** 2) * inside
    centre = extended[:, :, 1:-1]
    upward_diff = centre[:, 1:, :] - centre[:, :-1, :]
    upward = upward_diff / (1.0 + (upward_diff / edge_scale) ** 2)
    zeros_row = jnp.zeros_like(upward[:, :1, :])
    vertical = jnp.concatenate([upward, zeros_row], 1) - jnp.concatenate([zeros_row, upward], 1)
    return centre + smooth_rate * (sideways[:, :, 1:] - sideways[:, :, :-1] + vertical)


def per_device(
    granules,
    valid_rows,
    scene_order,
    intersections,
    row_resample,
    col_resample,
    w_in,
    w_hidden,
    w_out,
):
    scenes, group_bands, pixel_count = granules.shape
    side_cells = valid_rows.shape[1]
    top = intersections.shape[1]
    tile_count = lax.axis_size("tile")
    band_count = lax.axis_size("band")
    band = lax.axis_index("band")
    tile = lax.axis_index("tile")
    entry_count = scenes * top
    cap = (entry_count + tile_count - 1) // tile_count + 1
    part = pixel_count // band_count
    row_count = side_cells // band_count

    laid = granules.reshape(scenes, group_bands, pixel_count // 128, 128)
    quarters = jnp.stack([granules[:, :, b * part : (b + 1) * part] for b in range(band_count)])
    recency = jnp.exp(1.4 * scene_order.astype(F32) / (scenes * tile_count) - 0.7)
    valid_here = lax.dynamic_slice_in_dim(valid_rows, band * row_count, row_count, 1).astype(F32)
    scale = valid_here * recency[:, None]
    scale = jnp.broadcast_to(scale[:, :, None], (scenes, row_count, side_cells))
    scale = scale.reshape(scenes, part // 128, 128)
    flat_dest = intersections.reshape(entry_count)
    is_dest = flat_dest[None, :] == jnp.arange(tile_count, dtype=jnp.int32)[:, None]
    rank = jnp.cumsum(is_dest.astype(jnp.int32), 1) - 1
    pick = is_dest[:, None, :] & (rank[:, None, :] == jnp.arange(cap)[None, :, None])
    scene_ids = (jnp.arange(entry_count, dtype=jnp.int32) // top + 1)[None, None, :]
    code = jnp.sum(jnp.where(pick, scene_ids, 0), 2) - 1
    meta = jnp.zeros((tile_count, 8, 128), jnp.int32).at[:, 0, :cap].set(code)
    pick = pick.reshape(tile_count * cap, entry_count).astype(BF)
    both = jnp.concatenate(
        [
            lax.dynamic_slice_in_dim(m, band * part, part, 2).reshape(entry_count, part)
            for m in (row_resample, col_resample)
        ],
        1,
    )
    sent = jnp.dot(pick, both, preferred_element_type=F32).astype(BF)
    sent = sent.reshape(tile_count * cap, 2 * part // 128, 128)
    planes, weights, matrices, codes = exchange(
        quarters, laid, sent, meta, scale, w_in, w_hidden, w_out
    )
    estimate = merge(codes[:, 0, :cap].reshape(-1), planes, weights, matrices)
    field = estimate.reshape(side_cells, group_bands, side_cells).transpose(1, 0, 2)

    forward = [(i, i + 1) for i in range(tile_count - 1)]
    backward = [(i + 1, i) for i in range(tile_count - 1)]
    low = lax.ppermute(field[:, :, side_cells - SMOOTH :], "tile", forward)
    high = lax.ppermute(field[:, :, :SMOOTH], "tile", backward)
    field = jnp.concatenate([low, field, high], 2)
    for step in range(SMOOTH):
        first_col = tile * side_cells - SMOOTH + step
        field = smooth_step(field, first_col, tile_count * side_cells)
    return field.reshape(group_bands, pixel_count)


def solution(mesh):
    return jax.shard_map(
        per_device,
        mesh=mesh,
        in_specs=(
            P("tile", "band", None),
            P("tile", None),
            P("tile"),
            P("tile", None),
            P("tile", None, None),
            P("tile", None, None),
            P(),
            P(),
            P(),
        ),
        out_specs=P("band", "tile"),
        check_vma=False,
    )
```

```python
import functools

import jax
import jax.numpy as jnp
import numpy as np
from jax import lax
from jax.experimental import pallas as pl
from jax.experimental.pallas import tpu as pltpu
from jax.sharding import PartitionSpec as P

HUBER_ITERS = 4
SMOOTH = 2
prior_weight = 0.25
huber_delta = 0.5
smooth_rate = 0.2
BF = jnp.bfloat16
F32 = jnp.float32


def reproject_slot(r, slot, code_ref, x_ref, w_ref, m_ref, q_ref, y_ref, wt_ref):
    lane = lax.broadcasted_iota(jnp.int32, (32, 128), 1)
    low = lane < 64
    quarters = range(m_ref.shape[0])
    code = code_ref[0, r]
    scene = jnp.maximum(code, 0)
    present = jnp.minimum(code + 1, 1).astype(F32)
    planes = x_ref[scene]
    weight = jnp.concatenate([w_ref[b, scene] for b in quarters], axis=0)
    rows = jnp.concatenate([m_ref[b, r, 0:8] for b in quarters], axis=0)
    cols = jnp.concatenate([m_ref[b, r, 8:16] for b in quarters], axis=0).astype(F32)
    turned = pltpu.roll(cols, 64, 1)
    zero = jnp.zeros((32, 128), F32)
    first = jnp.concatenate([jnp.where(low, cols, zero), jnp.where(low, turned, zero)], 0)
    second = jnp.concatenate([jnp.where(low, zero, turned), jnp.where(low, zero, cols)], 0)
    first, second = first.astype(BF), second.astype(BF)
    blank = jnp.zeros((64, 128), BF)
    right = jnp.concatenate(
        [
            jnp.concatenate([first, blank], 1),
            jnp.concatenate([blank, first], 1),
            jnp.concatenate([second, blank], 1),
            jnp.concatenate([blank, second], 1),
        ],
        0,
    )
    left = jnp.concatenate(
        [
            jnp.concatenate([planes[0], planes[1]], 1),
            jnp.concatenate([planes[2], planes[3]], 1),
            jnp.concatenate([weight, weight], 1),
        ],
        0,
    )
    half = lax.dot_general(
        left, right, (((1,), (1,)), ((), ())), preferred_element_type=F32
    ).astype(BF)
    stacked = jnp.concatenate(
        [
            jnp.concatenate([half[p * 32 : p * 32 + 32, 0:128] for p in range(3)], 1),
            jnp.concatenate([half[p * 32 : p * 32 + 32, 128:256] for p in range(3)], 1),
        ],
        0,
    )
    spread = jnp.dot(rows, q_ref[...], preferred_element_type=F32).astype(BF)
    row_matrix = jnp.concatenate([spread[:, 0:64], spread[:, 128:192]], 0)
    moved = jnp.dot(row_matrix, stacked, preferred_element_type=F32).astype(BF).astype(F32)
    y_ref[slot] = moved[:, 0:256]
    wt_ref[slot] = moved[:, 256:384] * present


def robust_merge(y_ref, wt_ref, field_ref, u_ref, v_ref):
    slots = y_ref.shape[0]
    chunk = 16

    def merge_rows(i, carry):
        here = pl.ds(pl.multiple_of(i * chunk, chunk), chunk)

        def load(n):
            w = wt_ref[n, here, :]
            return y_ref[n, here, :], jnp.concatenate([w, w], 1)

        def plain(n, sums):
            y, w = load(n)
            return sums[0] + w * y, sums[1] + w

        def robust(estimate, n, sums):
            y, w = load(n)
            size = jnp.maximum(jnp.abs(y - estimate), huber_delta)
            h = w * pl.reciprocal(size, approx=True)
            return sums[0] + h * y, sums[1] + h

        empty = (jnp.zeros((chunk, 256), F32), jnp.zeros((chunk, 256), F32))
        top, bottom = lax.fori_loop(0, slots, plain, empty, unroll=4)
        estimate = top / (bottom + prior_weight)
        for _ in range(HUBER_ITERS):
            top, bottom = lax.fori_loop(
                0, slots, functools.partial(robust, estimate), empty, unroll=4
            )
            estimate = top / (bottom + prior_weight / huber_delta)
        field_ref[here, :] = estimate
        return carry

    lax.fori_loop(0, 64 // chunk, merge_rows, 0)
    exact = lax.Precision.HIGHEST
    ordered = jnp.dot(u_ref[...], field_ref[...], precision=exact, preferred_element_type=F32)
    for pair in range(2):
        here = slice(pair * 128, pair * 128 + 128)
        field_ref[:, here] = jnp.dot(
            ordered[:, here], v_ref[...], precision=exact, preferred_element_type=F32
        )


def order_matrices():
    q = np.zeros((128, 256), np.float32)
    u = np.zeros((64, 64), np.float32)
    v = np.zeros((128, 128), np.float32)
    for n in range(64):
        place = (n % 2) * 32 + n // 2
        q[n, place] = 1
        q[64 + n, 128 + place] = 1
        u[n, place] = 1
        v[place, n] = 1
        v[64 + place, 64 + n] = 1
    return jnp.asarray(q, BF), jnp.asarray(u), jnp.asarray(v)


MESH = pl.DeviceIdType.MESH


def exchange_kernel(
    segment,
    quarters_ref,
    laid_ref,
    sent_ref,
    meta_ref,
    scale_ref,
    w_in_ref,
    w_hid_ref,
    w_out_ref,
    q_ref,
    u_ref,
    v_ref,
    out_ref,
    planes_ref,
    weights_ref,
    matrices_ref,
    codes_ref,
    x_ref,
    own_ref,
    stage_x,
    stage_w,
    stage_m,
    stage_code,
    y_ref,
    wt_ref,
    field_ref,
    near_left,
    near_right,
    last_ref,
    local_sems,
    x_send,
    x_recv,
    right_send,
    left_send,
    plane_recv,
    mat_send,
    mat_recv,
    code_send,
    code_recv,
    weight_send,
    weight_recv,
    mat_band_send,
    mat_band_recv,
    weight_band_send,
    weight_band_recv,
    halo_send,
    halo_recv,
):
    tiles = planes_ref.shape[0]
    bands = quarters_ref.shape[0]
    scenes = laid_ref.shape[0]
    cap = sent_ref.shape[0] // tiles
    tile = lax.axis_index("tile")
    band = lax.axis_index("band")

    def tile_peer(k):
        return lax.rem(tile + k, tiles)

    def tile_source(k):
        return lax.rem(tile + tiles - k, tiles)

    def band_peer(k):
        return lax.rem(band + k, bands)

    def for_tiles(first, body):
        def step(k, carry):
            body(k)
            return carry

        lax.fori_loop(first, tiles, step, 0)

    barrier = pltpu.get_barrier_semaphore()
    for_tiles(
        1,
        lambda k: pl.semaphore_signal(
            barrier, inc=1, device_id={"tile": tile_peer(k)}, device_id_type=MESH
        ),
    )
    for k in range(1, bands):
        pl.semaphore_signal(barrier, inc=1, device_id={"band": band_peer(k)}, device_id_type=MESH)
    pl.semaphore_wait(barrier, tiles - 1 + bands - 1)

    def remote(src, dst, send, recv, where):
        return pltpu.make_async_remote_copy(
            src_ref=src,
            dst_ref=dst,
            send_sem=send,
            recv_sem=recv,
            device_id=where,
            device_id_type=MESH,
        )

    def x_copy(peer, source):
        return remote(
            quarters_ref.at[peer], x_ref.at[source], x_send.at[peer], x_recv.at[source],
            {"band": peer},
        )

    def plane_copy(shard, target, sems):
        return remote(
            planes_ref.at[shard], planes_ref.at[shard], sems.at[shard], plane_recv.at[shard],
            {"tile": target},
        )

    def own_plane_copy(target, sems):
        return remote(
            laid_ref, planes_ref.at[tile], sems.at[tile], plane_recv.at[tile], {"tile": target}
        )

    def mat_copy(peer, source):
        return remote(
            sent_ref.at[pl.ds(peer * cap, cap)], matrices_ref.at[band, source],
            mat_send.at[peer], mat_recv.at[source], {"tile": peer},
        )

    def code_copy(peer, source):
        return remote(
            meta_ref.at[peer], codes_ref.at[source], code_send.at[peer], code_recv.at[source],
            {"tile": peer},
        )

    def weight_copy(peer, source):
        return remote(
            own_ref, weights_ref.at[band, source], weight_send.at[peer], weight_recv.at[source],
            {"tile": peer},
        )

    def mat_band_copy(source, peer, owner):
        return remote(
            matrices_ref.at[owner, source], matrices_ref.at[owner, source],
            mat_band_send.at[peer], mat_band_recv.at[owner], {"band": peer},
        )

    def weight_band_copy(source, peer, owner):
        return remote(
            weights_ref.at[owner, source], weights_ref.at[owner, source],
            weight_band_send.at[peer], weight_band_recv.at[owner], {"band": peer},
        )

    for k in range(1, bands):
        x_copy(band_peer(k), band).start()
    x_local = pltpu.make_async_copy(quarters_ref.at[band], x_ref.at[band], local_sems.at[0])
    x_local.start()

    @pl.when(tile < tiles - 1)
    def _():
        own_plane_copy(tile + 1, right_send).start()

    @pl.when(tile > 0)
    def _():
        own_plane_copy(tile - 1, left_send).start()

    def first_sends(k):
        mat_copy(tile_peer(k), tile).start()
        code_copy(tile_peer(k), tile).start()

    for_tiles(1, first_sends)
    plane_local = pltpu.make_async_copy(laid_ref, planes_ref.at[tile], local_sems.at[1])
    plane_local.start()
    mat_local = pltpu.make_async_copy(
        sent_ref.at[pl.ds(tile * cap, cap)], matrices_ref.at[band, tile], local_sems.at[2]
    )
    mat_local.start()
    code_local = pltpu.make_async_copy(meta_ref.at[tile], codes_ref.at[tile], local_sems.at[3])
    code_local.start()

    def forward(s):
        left, right = tile - s, tile + s

        @pl.when(left >= 0)
        def _():
            plane_copy(left, tile, right_send).wait_recv()

            @pl.when(tile < tiles - 1)
            def _():
                plane_copy(left, tile + 1, right_send).start()

        @pl.when(right < tiles)
        def _():
            plane_copy(right, tile, left_send).wait_recv()

            @pl.when(tile > 0)
            def _():
                plane_copy(right, tile - 1, left_send).start()

    def network(scene, carry):
        def silu(t):
            return (t + t * jnp.tanh(t)).astype(BF)

        x = jnp.concatenate([x_ref[b, scene] for b in range(bands)], axis=0)
        hidden = silu(jnp.dot(w_in_ref[...], x, preferred_element_type=F32))
        for layer in range(w_hid_ref.shape[0]):
            hidden = silu(jnp.dot(w_hid_ref[layer], hidden, preferred_element_type=F32))
        logits = jnp.dot(w_out_ref[...], hidden, preferred_element_type=F32)
        row = jax.nn.sigmoid(-logits[0:1])
        pieces = [row[:, i * 128 : (i + 1) * 128] for i in range(row.shape[1] // 128)]
        own_ref[scene] = (jnp.concatenate(pieces, axis=0) * scale_ref[scene]).astype(BF)
        return carry

    def share_matrices():
        mat_local.wait()
        for k in range(1, bands):
            mat_band_copy(tile, band_peer(k), band).start()

        def share(k):
            source = tile_source(k)
            mat_copy(tile, source).wait_recv()
            for j in range(1, bands):
                mat_band_copy(source, band_peer(j), band).start()

        for_tiles(1, share)

    for k in range(1, bands):
        source = lax.rem(band + bands - k, bands)
        x_copy(source, source).wait_recv()
    x_local.wait()
    steps = 1
    for start in range(0, scenes, segment):
        lax.fori_loop(start, start + segment, network, 0)
        if steps < tiles:
            forward(steps)
            steps += 1
        if start == 2 * segment:
            share_matrices()

    weight_local = pltpu.make_async_copy(own_ref, weights_ref.at[band, tile], local_sems.at[4])
    weight_local.start()
    for_tiles(1, lambda k: weight_copy(tile_peer(k), tile).start())
    weight_local.wait()
    for k in range(1, bands):
        weight_band_copy(tile, band_peer(k), band).start()

    def share_weights(k):
        source = tile_source(k)
        weight_copy(tile, source).wait_recv()
        for j in range(1, bands):
            weight_band_copy(source, band_peer(j), band).start()

    if steps < tiles:
        forward(steps)
        steps += 1
    for_tiles(1, share_weights)
    plane_local.wait()
    code_local.wait()
    for_tiles(1, lambda k: code_copy(tile, tile_source(k)).wait_recv())
    for k in range(1, bands):
        peer = band_peer(k)
        for ref, send, recv in (
            (matrices_ref, mat_band_send, mat_band_recv),
            (weights_ref, weight_band_send, weight_band_recv),
        ):
            whole = remote(ref.at[peer], ref.at[peer], send.at[peer], recv.at[peer], {"band": peer})
            whole.wait_recv()

    def reproject(first, last):
        def turn(n, carry):
            source = tile + (n // 2) * (1 - 2 * (n % 2))

            @pl.when((source >= 0) & (source < tiles) & (n != 1))
            def _():
                copies = [
                    pltpu.make_async_copy(planes_ref.at[source], stage_x, local_sems.at[5]),
                    pltpu.make_async_copy(codes_ref.at[source], stage_code, local_sems.at[6]),
                ]
                for b in range(bands):
                    copies.append(
                        pltpu.make_async_copy(
                            weights_ref.at[b, source], stage_w.at[b], local_sems.at[7 + 2 * b]
                        )
                    )
                    copies.append(
                        pltpu.make_async_copy(
                            matrices_ref.at[b, source], stage_m.at[b], local_sems.at[8 + 2 * b]
                        )
                    )
                for copy in copies:
                    copy.start()
                for copy in copies:
                    copy.wait()
                for r in range(cap):
                    reproject_slot(
                        r, source * cap + r, stage_code, stage_x, stage_w, stage_m, q_ref, y_ref,
                        wt_ref,
                    )

            return carry

        lax.fori_loop(2 * first, 2 * last, turn, 0)

    if tiles <= 8:
        begun = 0
        for s in range(3, tiles, 3):
            reproject(begun, s)
            begun = s
            if steps < tiles:
                forward(steps)
                steps += 1
        for_tiles(steps, forward)
        reproject(begun, tiles)
    else:
        for_tiles(steps, forward)
        reproject(0, tiles)

    robust_merge(y_ref, wt_ref, field_ref, u_ref, v_ref)

    def halo(target, landing, way):
        return remote(
            field_ref, landing, halo_send.at[way], halo_recv.at[way], {"tile": target}
        )

    @pl.when(tile < tiles - 1)
    def _():
        halo(tile + 1, near_left, 0).start()

    @pl.when(tile > 0)
    def _():
        halo(tile - 1, near_right, 1).start()

    @pl.when(tile == 0)
    def _():
        near_left[...] = jnp.zeros_like(near_left)

    @pl.when(tile == tiles - 1)
    def _():
        near_right[...] = jnp.zeros_like(near_right)

    @pl.when(tile > 0)
    def _():
        halo(tile, near_left, 0).wait_recv()

    @pl.when(tile < tiles - 1)
    def _():
        halo(tile, near_right, 1).wait_recv()

    lane = lax.broadcasted_iota(jnp.int32, (64, 128), 1)
    line = lax.broadcasted_iota(jnp.int32, (64, 128), 0)
    shut = ((lane == 127) & (tile == 0)) | ((lane == 63) & (tile == tiles - 1))
    for c in range(out_ref.shape[0]):
        pair = pl.ds((c // 2) * 128, 128)
        own, low, high = field_ref[:, pair], near_left[:, pair], near_right[:, pair]
        if c % 2 == 0:
            low, high = pltpu.roll(low, 64, 1), pltpu.roll(high, 64, 1)
        else:
            own = pltpu.roll(own, 64, 1)
        g = jnp.where(lane < 64, own, jnp.where(lane < 96, high, low))
        for _ in range(SMOOTH):
            across = pltpu.roll(g, 127, 1) - g
            side = jnp.where(shut, 0.0, across / (1.0 + across * across))
            down = pltpu.roll(g, 63, 0) - g
            upright = jnp.where(line == 63, 0.0, down / (1.0 + down * down))
            g = g + smooth_rate * (
                side - pltpu.roll(side, 1, 1) + (upright - pltpu.roll(upright, 1, 0))
            )
        last_ref[c] = g
        even = last_ref[c, pl.ds(0, 32, stride=2), :]
        odd = last_ref[c, pl.ds(1, 32, stride=2), :]
        out_ref[c] = jnp.where(lane[:32] < 64, even, pltpu.roll(odd, 64, 1))

    @pl.when(tile < tiles - 1)
    def _():
        halo(tile + 1, near_left, 0).wait_send()

    @pl.when(tile > 0)
    def _():
        halo(tile - 1, near_right, 1).wait_send()

    def finish(k):
        code_copy(tile_peer(k), tile).wait_send()
        mat_copy(tile_peer(k), tile).wait_send()
        weight_copy(tile_peer(k), tile).wait_send()

    for_tiles(1, finish)

    def finish_planes(shard):
        @pl.when((shard <= tile) & (tile < tiles - 1))
        def _():
            plane_copy(shard, tile, right_send).wait_send()

        @pl.when((shard >= tile) & (tile > 0))
        def _():
            plane_copy(shard, tile, left_send).wait_send()

    for_tiles(0, finish_planes)
    for k in range(1, bands):
        peer = band_peer(k)
        x_copy(peer, band).wait_send()
        for ref, send, recv in (
            (matrices_ref, mat_band_send, mat_band_recv),
            (weights_ref, weight_band_send, weight_band_recv),
        ):
            whole = remote(ref.at[peer], ref.at[peer], send.at[peer], recv.at[peer], {"band": peer})
            whole.wait_send()


def exchange(quarters, laid, sent, meta, scale, w_in, w_hidden, w_out):
    bands, scenes, part, width = quarters.shape
    tiles = meta.shape[0]
    cap = sent.shape[0] // tiles
    hid = w_in.shape[1]
    layers = w_hidden.shape[0]
    half = jnp.asarray(0.5, BF)
    w_in_t = (w_in * half).T
    w_hid_t = jnp.swapaxes(w_hidden * half, 1, 2)
    w_out_t = jnp.broadcast_to(w_out[None, :], (16, hid))
    lines = width // 128
    anywhere = pl.BlockSpec(memory_space=pl.ANY)
    vmem = pl.BlockSpec(memory_space=pltpu.VMEM)
    dma = pltpu.SemaphoreType.DMA
    return pl.pallas_call(
        functools.partial(exchange_kernel, max(1, scenes // 4)),
        in_specs=[anywhere] * 4 + [vmem] * 7,
        out_specs=[vmem] + [anywhere] * 4,
        out_shape=[
            jax.ShapeDtypeStruct(laid.shape[1:], F32),
            jax.ShapeDtypeStruct((tiles,) + laid.shape, BF),
            jax.ShapeDtypeStruct((bands, tiles, scenes, lines, 128), BF),
            jax.ShapeDtypeStruct((bands, tiles, cap) + sent.shape[1:], BF),
            jax.ShapeDtypeStruct(meta.shape, jnp.int32),
        ],
        scratch_shapes=[
            pltpu.VMEM(quarters.shape, BF),
            pltpu.VMEM((scenes, lines, 128), BF),
            pltpu.VMEM(laid.shape, BF),
            pltpu.VMEM((bands, scenes, lines, 128), BF),
            pltpu.VMEM((bands, cap) + sent.shape[1:], BF),
            pltpu.SMEM(meta.shape[1:], jnp.int32),
            pltpu.VMEM((tiles * cap, 64, 256), F32),
            pltpu.VMEM((tiles * cap, 64, 128), F32),
            pltpu.VMEM((64, 256), F32),
            pltpu.VMEM((64, 256), F32),
            pltpu.VMEM((64, 256), F32),
            pltpu.VMEM((part, 64, 128), F32),
            dma((7 + 2 * bands,)),
            dma((bands,)),
            dma((bands,)),
        ]
        + [dma((tiles,))] * 9
        + [dma((bands,))] * 4
        + [dma((2,))] * 2,
        compiler_params=pltpu.CompilerParams(
            collective_id=0, has_side_effects=True, vmem_limit_bytes=32 * 1024 * 1024
        ),
    )(quarters, laid, sent, meta, scale, w_in_t, w_hid_t, w_out_t, *order_matrices())[0]


def per_device(
    granules,
    valid_rows,
    scene_order,
    intersections,
    row_resample,
    col_resample,
    w_in,
    w_hidden,
    w_out,
):
    scenes, group_bands, pixel_count = granules.shape
    side_cells = valid_rows.shape[1]
    top = intersections.shape[1]
    tile_count = lax.axis_size("tile")
    band_count = lax.axis_size("band")
    band = lax.axis_index("band")
    tile = lax.axis_index("tile")
    entry_count = scenes * top
    cap = (entry_count + tile_count - 1) // tile_count + 1
    part = pixel_count // band_count
    row_count = side_cells // band_count

    laid = granules.reshape(scenes, group_bands, pixel_count // 128, 128)
    quarters = jnp.stack([granules[:, :, b * part : (b + 1) * part] for b in range(band_count)])
    recency = jnp.exp(1.4 * scene_order.astype(F32) / (scenes * tile_count) - 0.7)
    valid_here = lax.dynamic_slice_in_dim(valid_rows, band * row_count, row_count, 1).astype(F32)
    scale = valid_here * recency[:, None]
    scale = jnp.broadcast_to(scale[:, :, None], (scenes, row_count, side_cells))
    scale = scale.reshape(scenes, part // 128, 128)
    flat_dest = intersections.reshape(entry_count)
    is_dest = flat_dest[None, :] == jnp.arange(tile_count, dtype=jnp.int32)[:, None]
    rank = jnp.cumsum(is_dest.astype(jnp.int32), 1) - 1
    pick = is_dest[:, None, :] & (rank[:, None, :] == jnp.arange(cap)[None, :, None])
    scene_ids = (jnp.arange(entry_count, dtype=jnp.int32) // top + 1)[None, None, :]
    code = jnp.sum(jnp.where(pick, scene_ids, 0), 2) - 1
    meta = jnp.zeros((tile_count, 8, 128), jnp.int32).at[:, 0, :cap].set(code)
    pick = pick.reshape(tile_count * cap, entry_count).astype(BF)
    both = jnp.concatenate(
        [
            lax.dynamic_slice_in_dim(m, band * part, part, 2).reshape(entry_count, part)
            for m in (row_resample, col_resample)
        ],
        1,
    )
    sent = jnp.dot(pick, both, preferred_element_type=F32).astype(BF)
    sent = sent.reshape(tile_count * cap, 2 * part // 128, 128)
    field = exchange(quarters, laid, sent, meta, scale, w_in, w_hidden, w_out)
    return field.reshape(group_bands, pixel_count)


def solution(mesh):
    return jax.shard_map(
        per_device,
        mesh=mesh,
        in_specs=(
            P("tile", "band", None),
            P("tile", None),
            P("tile"),
            P("tile", None),
            P("tile", None, None),
            P("tile", None, None),
            P(),
            P(),
            P(),
        ),
        out_specs=P("band", "tile"),
        check_vma=False,
    )
```

```python
import functools

import jax
import jax.numpy as jnp
import numpy as np
from jax import lax
from jax.experimental import pallas as pl
from jax.experimental.pallas import tpu as pltpu
from jax.sharding import PartitionSpec as P

HUBER_ITERS = 4
SMOOTH = 2
prior_weight = 0.25
huber_delta = 0.5
smooth_rate = 0.2
BF = jnp.bfloat16
F32 = jnp.float32


def reproject_slot(r, slot, code_ref, x_ref, w_ref, m_ref, q_ref, y_ref, wt_ref):
    lane = lax.broadcasted_iota(jnp.int32, (32, 128), 1)
    low = lane < 64
    quarters = range(m_ref.shape[0])
    code = code_ref[0, r]
    scene = jnp.maximum(code, 0)
    present = jnp.minimum(code + 1, 1).astype(F32)
    planes = x_ref[scene]
    weight = jnp.concatenate([w_ref[b, scene] for b in quarters], axis=0)
    rows = jnp.concatenate([m_ref[b, r, 0:8] for b in quarters], axis=0)
    cols = jnp.concatenate([m_ref[b, r, 8:16] for b in quarters], axis=0).astype(F32)
    turned = pltpu.roll(cols, 64, 1)
    zero = jnp.zeros((32, 128), F32)
    first = jnp.concatenate([jnp.where(low, cols, zero), jnp.where(low, turned, zero)], 0)
    second = jnp.concatenate([jnp.where(low, zero, turned), jnp.where(low, zero, cols)], 0)
    first, second = first.astype(BF), second.astype(BF)
    blank = jnp.zeros((64, 128), BF)
    right = jnp.concatenate(
        [
            jnp.concatenate([first, blank], 1),
            jnp.concatenate([blank, first], 1),
            jnp.concatenate([second, blank], 1),
            jnp.concatenate([blank, second], 1),
        ],
        0,
    )
    left = jnp.concatenate(
        [
            jnp.concatenate([planes[0], planes[1]], 1),
            jnp.concatenate([planes[2], planes[3]], 1),
            jnp.concatenate([weight, weight], 1),
        ],
        0,
    )
    half = lax.dot_general(
        left, right, (((1,), (1,)), ((), ())), preferred_element_type=F32
    ).astype(BF)
    stacked = jnp.concatenate(
        [
            jnp.concatenate([half[p * 32 : p * 32 + 32, 0:128] for p in range(3)], 1),
            jnp.concatenate([half[p * 32 : p * 32 + 32, 128:256] for p in range(3)], 1),
        ],
        0,
    )
    spread = jnp.dot(rows, q_ref[...], preferred_element_type=F32).astype(BF)
    row_matrix = jnp.concatenate([spread[:, 0:64], spread[:, 128:192]], 0)
    moved = jnp.dot(row_matrix, stacked, preferred_element_type=F32).astype(BF).astype(F32)
    y_ref[slot] = moved[:, 0:256]
    wt_ref[slot] = moved[:, 256:384] * present


def robust_merge(y_ref, wt_ref, field_ref, u_ref, v_ref):
    slots = y_ref.shape[0]
    chunk = 16

    def merge_rows(i, carry):
        here = pl.ds(pl.multiple_of(i * chunk, chunk), chunk)

        def load(n):
            w = wt_ref[n, here, :]
            return y_ref[n, here, :], jnp.concatenate([w, w], 1)

        def plain(n, sums):
            y, w = load(n)
            return sums[0] + w * y, sums[1] + w

        def robust(estimate, n, sums):
            y, w = load(n)
            size = jnp.maximum(jnp.abs(y - estimate), huber_delta)
            h = w * pl.reciprocal(size, approx=True)
            return sums[0] + h * y, sums[1] + h

        empty = (jnp.zeros((chunk, 256), F32), jnp.zeros((chunk, 256), F32))
        top, bottom = lax.fori_loop(0, slots, plain, empty, unroll=4)
        estimate = top / (bottom + prior_weight)
        for _ in range(HUBER_ITERS):
            top, bottom = lax.fori_loop(
                0, slots, functools.partial(robust, estimate), empty, unroll=4
            )
            estimate = top / (bottom + prior_weight / huber_delta)
        field_ref[here, :] = estimate
        return carry

    lax.fori_loop(0, 64 // chunk, merge_rows, 0)
    exact = lax.Precision.HIGHEST
    ordered = jnp.dot(u_ref[...], field_ref[...], precision=exact, preferred_element_type=F32)
    for pair in range(2):
        here = slice(pair * 128, pair * 128 + 128)
        field_ref[:, here] = jnp.dot(
            ordered[:, here], v_ref[...], precision=exact, preferred_element_type=F32
        )


def order_matrices():
    q = np.zeros((128, 256), np.float32)
    u = np.zeros((64, 64), np.float32)
    v = np.zeros((128, 128), np.float32)
    for n in range(64):
        place = (n % 2) * 32 + n // 2
        q[n, place] = 1
        q[64 + n, 128 + place] = 1
        u[n, place] = 1
        v[place, n] = 1
        v[64 + place, 64 + n] = 1
    return jnp.asarray(q, BF), jnp.asarray(u), jnp.asarray(v)


MESH = pl.DeviceIdType.MESH


def exchange_kernel(
    quarters_ref,
    laid_ref,
    sent_ref,
    meta_ref,
    valid_ref,
    order_ref,
    w_in_raw,
    w_hid_raw,
    w_out_raw,
    q_ref,
    u_ref,
    v_ref,
    out_ref,
    planes_ref,
    weights_ref,
    matrices_ref,
    codes_ref,
    x_ref,
    own_ref,
    w_in_ref,
    w_hid_ref,
    stage_x,
    stage_w,
    stage_m,
    stage_code,
    y_ref,
    wt_ref,
    field_ref,
    near_left,
    near_right,
    last_ref,
    local_sems,
    x_send,
    x_recv,
    right_send,
    left_send,
    plane_recv,
    mat_send,
    mat_recv,
    code_send,
    code_recv,
    weight_send,
    weight_recv,
    mat_band_send,
    mat_band_recv,
    weight_band_send,
    weight_band_recv,
    halo_send,
    halo_recv,
):
    tiles = planes_ref.shape[0]
    bands = quarters_ref.shape[0]
    scenes = laid_ref.shape[0]
    cap = sent_ref.shape[0] // tiles
    tile = lax.axis_index("tile")
    band = lax.axis_index("band")

    def tile_peer(k):
        return lax.rem(tile + k, tiles)

    def tile_source(k):
        return lax.rem(tile + tiles - k, tiles)

    def band_peer(k):
        return lax.rem(band + k, bands)

    def for_tiles(first, body):
        def step(k, carry):
            body(k)
            return carry

        lax.fori_loop(first, tiles, step, 0)

    barrier = pltpu.get_barrier_semaphore()
    for_tiles(
        1,
        lambda k: pl.semaphore_signal(
            barrier, inc=1, device_id={"tile": tile_peer(k)}, device_id_type=MESH
        ),
    )
    for k in range(1, bands):
        pl.semaphore_signal(barrier, inc=1, device_id={"band": band_peer(k)}, device_id_type=MESH)
    pl.semaphore_wait(barrier, tiles - 1 + bands - 1)

    def remote(src, dst, send, recv, where):
        return pltpu.make_async_remote_copy(
            src_ref=src,
            dst_ref=dst,
            send_sem=send,
            recv_sem=recv,
            device_id=where,
            device_id_type=MESH,
        )

    def x_copy(peer, source):
        return remote(
            quarters_ref.at[peer], x_ref.at[source], x_send.at[peer], x_recv.at[source],
            {"band": peer},
        )

    def plane_copy(shard, target, sems):
        return remote(
            planes_ref.at[shard], planes_ref.at[shard], sems.at[shard], plane_recv.at[shard],
            {"tile": target},
        )

    def own_plane_copy(target, sems):
        return remote(
            laid_ref, planes_ref.at[tile], sems.at[tile], plane_recv.at[tile], {"tile": target}
        )

    def mat_copy(peer, source):
        return remote(
            sent_ref.at[pl.ds(peer * cap, cap)], matrices_ref.at[band, source],
            mat_send.at[peer], mat_recv.at[source], {"tile": peer},
        )

    def code_copy(peer, source):
        return remote(
            meta_ref.at[peer], codes_ref.at[source], code_send.at[peer], code_recv.at[source],
            {"tile": peer},
        )

    def weight_copy(peer, source):
        return remote(
            own_ref, weights_ref.at[band, source], weight_send.at[peer], weight_recv.at[source],
            {"tile": peer},
        )

    def mat_band_copy(source, peer, owner):
        return remote(
            matrices_ref.at[owner, source], matrices_ref.at[owner, source],
            mat_band_send.at[peer], mat_band_recv.at[owner], {"band": peer},
        )

    def weight_band_copy(source, peer, owner):
        return remote(
            weights_ref.at[owner, source], weights_ref.at[owner, source],
            weight_band_send.at[peer], weight_band_recv.at[owner], {"band": peer},
        )

    for k in range(1, bands):
        x_copy(band_peer(k), band).start()
    x_local = pltpu.make_async_copy(quarters_ref.at[band], x_ref.at[band], local_sems.at[0])
    x_local.start()

    @pl.when(tile < tiles - 1)
    def _():
        own_plane_copy(tile + 1, right_send).start()

    @pl.when(tile > 0)
    def _():
        own_plane_copy(tile - 1, left_send).start()

    def first_sends(k):
        mat_copy(tile_peer(k), tile).start()
        code_copy(tile_peer(k), tile).start()

    for_tiles(1, first_sends)
    plane_local = pltpu.make_async_copy(laid_ref, planes_ref.at[tile], local_sems.at[1])
    plane_local.start()
    mat_local = pltpu.make_async_copy(
        sent_ref.at[pl.ds(tile * cap, cap)], matrices_ref.at[band, tile], local_sems.at[2]
    )
    mat_local.start()
    code_local = pltpu.make_async_copy(meta_ref.at[tile], codes_ref.at[tile], local_sems.at[3])
    code_local.start()

    def forward(s):
        left, right = tile - s, tile + s

        @pl.when((left >= 0) & (tile < tiles - 1))
        def _():
            plane_copy(left, tile, right_send).wait_recv()
            plane_copy(left, tile + 1, right_send).start()

        @pl.when((right < tiles) & (tile > 0))
        def _():
            plane_copy(right, tile, left_send).wait_recv()
            plane_copy(right, tile - 1, left_send).start()

    def arrive(source):
        @pl.when((tile == 0) | (tile == tiles - 1))
        def _():
            plane_copy(source, tile, right_send).wait_recv()

    def network(scene, carry):
        def silu(t):
            return (t + t * jnp.tanh(t)).astype(BF)

        x = jnp.concatenate([x_ref[b, scene] for b in range(bands)], axis=0)
        hidden = silu(jnp.dot(w_in_ref[...], x, preferred_element_type=F32))
        for layer in range(w_hid_ref.shape[0]):
            hidden = silu(jnp.dot(w_hid_ref[layer], hidden, preferred_element_type=F32))
        w_out = jnp.broadcast_to(w_out_raw[...].astype(F32), (16, w_out_raw.shape[1]))
        logits = jnp.dot(w_out.astype(BF), hidden, preferred_element_type=F32)
        row = jax.nn.sigmoid(-logits[0:1])
        pieces = [row[:, i * 128 : (i + 1) * 128] for i in range(row.shape[1] // 128)]
        shape = (len(pieces), 128)
        line = lax.broadcasted_iota(jnp.int32, shape, 0)
        lane = lax.broadcasted_iota(jnp.int32, shape, 1)
        valid = jnp.zeros(shape, F32)
        side = 2 * len(pieces)
        for i in range(side):
            here = (line == i // 2) & (lane // 64 == i % 2)
            valid = jnp.where(here, valid_ref[scene, band * side + i].astype(F32), valid)
        order = jnp.full(shape, order_ref[scene], jnp.int32).astype(F32)
        recency = jnp.exp(1.4 * order / (scenes * tiles) - 0.7)
        own_ref[scene] = (jnp.concatenate(pieces, axis=0) * valid * recency).astype(BF)
        return carry

    def share_matrices():
        mat_local.wait()
        for k in range(1, bands):
            mat_band_copy(tile, band_peer(k), band).start()

        def share(k):
            source = tile_source(k)
            mat_copy(tile, source).wait_recv()
            for j in range(1, bands):
                mat_band_copy(source, band_peer(j), band).start()

        for_tiles(1, share)

    w_in_ref[...] = (w_in_raw[...].astype(F32) * 0.5).T.astype(BF)
    for layer in range(w_hid_raw.shape[0]):
        w_hid_ref[layer] = (w_hid_raw[layer].astype(F32) * 0.5).T.astype(BF)
    for k in range(1, bands):
        source = lax.rem(band + bands - k, bands)
        x_copy(source, source).wait_recv()
    x_local.wait()
    steps = 1
    for first, last in ((0, 3), (3, 7), (7, 13), (13, 16)):
        if steps < min(4, tiles):
            forward(steps)
            steps += 1
        if first == 7:
            share_matrices()
        lax.fori_loop(first * scenes // 16, last * scenes // 16, network, 0)

    weight_local = pltpu.make_async_copy(own_ref, weights_ref.at[band, tile], local_sems.at[4])
    weight_local.start()
    for_tiles(1, lambda k: weight_copy(tile_peer(k), tile).start())
    weight_local.wait()
    for k in range(1, bands):
        weight_band_copy(tile, band_peer(k), band).start()

    def share_weights(k):
        source = tile_source(k)
        weight_copy(tile, source).wait_recv()
        for j in range(1, bands):
            weight_band_copy(source, band_peer(j), band).start()

    if steps < tiles:
        forward(steps)
        steps += 1
    for_tiles(1, share_weights)
    if steps < tiles:
        forward(steps)
        steps += 1
    plane_local.wait()
    code_local.wait()
    for_tiles(1, lambda k: code_copy(tile, tile_source(k)).wait_recv())
    for k in range(1, bands):
        peer = band_peer(k)
        for ref, send, recv in (
            (matrices_ref, mat_band_send, mat_band_recv),
            (weights_ref, weight_band_send, weight_band_recv),
        ):
            whole = remote(ref.at[peer], ref.at[peer], send.at[peer], recv.at[peer], {"band": peer})
            whole.wait_recv()

    def reproject(first, last):
        def turn(n, carry):
            source = tile + (n // 2) * (1 - 2 * (n % 2))

            @pl.when((source >= 0) & (source < tiles) & (n != 1))
            def _():
                @pl.when(n > 0)
                def _():
                    arrive(source)

                copies = [
                    pltpu.make_async_copy(planes_ref.at[source], stage_x, local_sems.at[5]),
                    pltpu.make_async_copy(codes_ref.at[source], stage_code, local_sems.at[6]),
                ]
                for b in range(bands):
                    copies.append(
                        pltpu.make_async_copy(
                            weights_ref.at[b, source], stage_w.at[b], local_sems.at[7 + 2 * b]
                        )
                    )
                    copies.append(
                        pltpu.make_async_copy(
                            matrices_ref.at[b, source], stage_m.at[b], local_sems.at[8 + 2 * b]
                        )
                    )
                for copy in copies:
                    copy.start()
                for copy in copies:
                    copy.wait()
                for r in range(cap):
                    reproject_slot(
                        r, source * cap + r, stage_code, stage_x, stage_w, stage_m, q_ref, y_ref,
                        wt_ref,
                    )

            return carry

        lax.fori_loop(2 * first, 2 * last, turn, 0)

    if tiles <= 8:
        begun = 0
        for s in range(3, tiles, 3):
            reproject(begun, s)
            begun = s
            if steps < tiles:
                forward(steps)
                steps += 1
        for_tiles(steps, forward)
        reproject(begun, tiles)
    else:
        for_tiles(steps, forward)
        reproject(0, tiles)

    robust_merge(y_ref, wt_ref, field_ref, u_ref, v_ref)

    def halo(target, landing, way):
        return remote(
            field_ref, landing, halo_send.at[way], halo_recv.at[way], {"tile": target}
        )

    @pl.when(tile < tiles - 1)
    def _():
        halo(tile + 1, near_left, 0).start()

    @pl.when(tile > 0)
    def _():
        halo(tile - 1, near_right, 1).start()

    @pl.when(tile == 0)
    def _():
        near_left[...] = jnp.zeros_like(near_left)

    @pl.when(tile == tiles - 1)
    def _():
        near_right[...] = jnp.zeros_like(near_right)

    @pl.when(tile > 0)
    def _():
        halo(tile, near_left, 0).wait_recv()

    @pl.when(tile < tiles - 1)
    def _():
        halo(tile, near_right, 1).wait_recv()

    lane = lax.broadcasted_iota(jnp.int32, (64, 128), 1)
    line = lax.broadcasted_iota(jnp.int32, (64, 128), 0)
    shut = ((lane == 127) & (tile == 0)) | ((lane == 63) & (tile == tiles - 1))
    for c in range(out_ref.shape[0]):
        pair = pl.ds((c // 2) * 128, 128)
        own, low, high = field_ref[:, pair], near_left[:, pair], near_right[:, pair]
        if c % 2 == 0:
            low, high = pltpu.roll(low, 64, 1), pltpu.roll(high, 64, 1)
        else:
            own = pltpu.roll(own, 64, 1)
        g = jnp.where(lane < 64, own, jnp.where(lane < 96, high, low))
        for _ in range(SMOOTH):
            across = pltpu.roll(g, 127, 1) - g
            side = jnp.where(shut, 0.0, across / (1.0 + across * across))
            down = pltpu.roll(g, 63, 0) - g
            upright = jnp.where(line == 63, 0.0, down / (1.0 + down * down))
            g = g + smooth_rate * (
                side - pltpu.roll(side, 1, 1) + (upright - pltpu.roll(upright, 1, 0))
            )
        last_ref[c] = g
        even = last_ref[c, pl.ds(0, 32, stride=2), :]
        odd = last_ref[c, pl.ds(1, 32, stride=2), :]
        out_ref[c] = jnp.where(lane[:32] < 64, even, pltpu.roll(odd, 64, 1))

    @pl.when(tile < tiles - 1)
    def _():
        halo(tile + 1, near_left, 0).wait_send()

    @pl.when(tile > 0)
    def _():
        halo(tile - 1, near_right, 1).wait_send()

    def finish(k):
        code_copy(tile_peer(k), tile).wait_send()
        mat_copy(tile_peer(k), tile).wait_send()
        weight_copy(tile_peer(k), tile).wait_send()

    for_tiles(1, finish)

    def finish_planes(shard):
        @pl.when((shard <= tile) & (tile < tiles - 1))
        def _():
            plane_copy(shard, tile, right_send).wait_send()

        @pl.when((shard >= tile) & (tile > 0))
        def _():
            plane_copy(shard, tile, left_send).wait_send()

    for_tiles(0, finish_planes)
    for k in range(1, bands):
        peer = band_peer(k)
        x_copy(peer, band).wait_send()
        for ref, send, recv in (
            (matrices_ref, mat_band_send, mat_band_recv),
            (weights_ref, weight_band_send, weight_band_recv),
        ):
            whole = remote(ref.at[peer], ref.at[peer], send.at[peer], recv.at[peer], {"band": peer})
            whole.wait_send()


def exchange(quarters, laid, sent, meta, valid_rows, scene_order, w_in, w_hidden, w_out):
    bands, scenes, part, width = quarters.shape
    tiles = meta.shape[0]
    cap = sent.shape[0] // tiles
    hid = w_in.shape[1]
    layers = w_hidden.shape[0]
    lines = width // 128
    anywhere = pl.BlockSpec(memory_space=pl.ANY)
    vmem = pl.BlockSpec(memory_space=pltpu.VMEM)
    smem = pl.BlockSpec(memory_space=pltpu.SMEM)
    dma = pltpu.SemaphoreType.DMA
    return pl.pallas_call(
        exchange_kernel,
        in_specs=[anywhere] * 4 + [smem] * 2 + [vmem] * 6,
        out_specs=[vmem] + [anywhere] * 4,
        out_shape=[
            jax.ShapeDtypeStruct(laid.shape[1:], F32),
            jax.ShapeDtypeStruct((tiles,) + laid.shape, BF),
            jax.ShapeDtypeStruct((bands, tiles, scenes, lines, 128), BF),
            jax.ShapeDtypeStruct((bands, tiles, cap) + sent.shape[1:], BF),
            jax.ShapeDtypeStruct(meta.shape, jnp.int32),
        ],
        scratch_shapes=[
            pltpu.VMEM(quarters.shape, BF),
            pltpu.VMEM((scenes, lines, 128), BF),
            pltpu.VMEM((hid, bands * part), BF),
            pltpu.VMEM((layers, hid, hid), BF),
            pltpu.VMEM(laid.shape, BF),
            pltpu.VMEM((bands, scenes, lines, 128), BF),
            pltpu.VMEM((bands, cap) + sent.shape[1:], BF),
            pltpu.SMEM(meta.shape[1:], jnp.int32),
            pltpu.VMEM((tiles * cap, 64, 256), F32),
            pltpu.VMEM((tiles * cap, 64, 128), F32),
            pltpu.VMEM((64, 256), F32),
            pltpu.VMEM((64, 256), F32),
            pltpu.VMEM((64, 256), F32),
            pltpu.VMEM((part, 64, 128), F32),
            dma((7 + 2 * bands,)),
            dma((bands,)),
            dma((bands,)),
        ]
        + [dma((tiles,))] * 9
        + [dma((bands,))] * 4
        + [dma((2,))] * 2,
        compiler_params=pltpu.CompilerParams(
            collective_id=0, has_side_effects=True, vmem_limit_bytes=32 * 1024 * 1024
        ),
    )(
        quarters, laid, sent, meta, valid_rows, scene_order, w_in, w_hidden, w_out[None, :],
        *order_matrices(),
    )[0]


def per_device(
    granules,
    valid_rows,
    scene_order,
    intersections,
    row_resample,
    col_resample,
    w_in,
    w_hidden,
    w_out,
):
    scenes, group_bands, pixel_count = granules.shape
    top = intersections.shape[1]
    tile_count = lax.axis_size("tile")
    band_count = lax.axis_size("band")
    band = lax.axis_index("band")
    tile = lax.axis_index("tile")
    entry_count = scenes * top
    cap = (entry_count + tile_count - 1) // tile_count + 1
    part = pixel_count // band_count

    laid = granules.reshape(scenes, group_bands, pixel_count // 128, 128)
    quarters = jnp.stack([granules[:, :, b * part : (b + 1) * part] for b in range(band_count)])
    flat_dest = intersections.reshape(entry_count)
    is_dest = flat_dest[None, :] == jnp.arange(tile_count, dtype=jnp.int32)[:, None]
    rank = jnp.cumsum(is_dest.astype(jnp.int32), 1) - 1
    pick = is_dest[:, None, :] & (rank[:, None, :] == jnp.arange(cap)[None, :, None])
    scene_ids = (jnp.arange(entry_count, dtype=jnp.int32) // top + 1)[None, None, :]
    code = jnp.sum(jnp.where(pick, scene_ids, 0), 2) - 1
    meta = jnp.zeros((tile_count, 8, 128), jnp.int32).at[:, 0, :cap].set(code)
    pick = pick.reshape(tile_count * cap, entry_count).astype(BF)
    both = jnp.concatenate(
        [
            lax.dynamic_slice_in_dim(m, band * part, part, 2).reshape(entry_count, part)
            for m in (row_resample, col_resample)
        ],
        1,
    )
    sent = jnp.dot(pick, both, preferred_element_type=F32).astype(BF)
    sent = sent.reshape(tile_count * cap, 2 * part // 128, 128)
    field = exchange(
        quarters, laid, sent, meta, valid_rows, scene_order, w_in, w_hidden, w_out
    )
    return field.reshape(group_bands, pixel_count)


def solution(mesh):
    return jax.shard_map(
        per_device,
        mesh=mesh,
        in_specs=(
            P("tile", "band", None),
            P("tile", None),
            P("tile"),
            P("tile", None),
            P("tile", None, None),
            P("tile", None, None),
            P(),
            P(),
            P(),
        ),
        out_specs=P("band", "tile"),
        check_vma=False,
    )
```

```python
import functools

import jax
import jax.numpy as jnp
import numpy as np
from jax import lax
from jax.experimental import pallas as pl
from jax.experimental.pallas import tpu as pltpu
from jax.sharding import PartitionSpec as P

HUBER_ITERS = 4
SMOOTH = 2
prior_weight = 0.25
huber_delta = 0.5
smooth_rate = 0.2
BF = jnp.bfloat16
F32 = jnp.float32


def reproject_slot(r, cap, source, code_ref, x_ref, w_ref, m_ref, q_ref, y_ref, wt_ref):
    slot = source * cap + r
    side, place = lax.rem(source, 2), source // 2
    lane = lax.broadcasted_iota(jnp.int32, (32, 128), 1)
    low = lane < 64
    quarters = range(m_ref.shape[0])
    code = code_ref[source, 0, r]
    scene = jnp.maximum(code, 0)
    present = jnp.minimum(code + 1, 1).astype(F32)
    planes = x_ref[scene]
    weight = jnp.concatenate([w_ref[b, side, place, scene] for b in quarters], axis=0)
    rows = jnp.concatenate([m_ref[b, source, r, 0:8] for b in quarters], axis=0)
    cols = jnp.concatenate([m_ref[b, source, r, 8:16] for b in quarters], axis=0).astype(F32)
    turned = pltpu.roll(cols, 64, 1)
    zero = jnp.zeros((32, 128), F32)
    first = jnp.concatenate([jnp.where(low, cols, zero), jnp.where(low, turned, zero)], 0)
    second = jnp.concatenate([jnp.where(low, zero, turned), jnp.where(low, zero, cols)], 0)
    first, second = first.astype(BF), second.astype(BF)
    blank = jnp.zeros((64, 128), BF)
    right = jnp.concatenate(
        [
            jnp.concatenate([first, blank], 1),
            jnp.concatenate([blank, first], 1),
            jnp.concatenate([second, blank], 1),
            jnp.concatenate([blank, second], 1),
        ],
        0,
    )
    left = jnp.concatenate(
        [
            jnp.concatenate([planes[0], planes[1]], 1),
            jnp.concatenate([planes[2], planes[3]], 1),
            jnp.concatenate([weight, weight], 1),
        ],
        0,
    )
    half = lax.dot_general(
        left, right, (((1,), (1,)), ((), ())), preferred_element_type=F32
    ).astype(BF)
    stacked = jnp.concatenate(
        [
            jnp.concatenate([half[p * 32 : p * 32 + 32, 0:128] for p in range(3)], 1),
            jnp.concatenate([half[p * 32 : p * 32 + 32, 128:256] for p in range(3)], 1),
        ],
        0,
    )
    spread = jnp.dot(rows, q_ref[...], preferred_element_type=F32).astype(BF)
    row_matrix = jnp.concatenate([spread[:, 0:64], spread[:, 128:192]], 0)
    moved = jnp.dot(row_matrix, stacked, preferred_element_type=F32).astype(BF).astype(F32)
    y_ref[slot] = moved[:, 0:256]
    wt_ref[slot] = moved[:, 256:384] * present


def robust_merge(y_ref, wt_ref, field_ref, u_ref, v_ref):
    slots = y_ref.shape[0]
    chunk = 16

    def merge_rows(i, carry):
        here = pl.ds(pl.multiple_of(i * chunk, chunk), chunk)

        def load(n):
            w = wt_ref[n, here, :]
            return y_ref[n, here, :], jnp.concatenate([w, w], 1)

        def plain(n, sums):
            y, w = load(n)
            return sums[0] + w * y, sums[1] + w

        def robust(estimate, n, sums):
            y, w = load(n)
            size = jnp.maximum(jnp.abs(y - estimate), huber_delta)
            h = w * pl.reciprocal(size, approx=True)
            return sums[0] + h * y, sums[1] + h

        empty = (jnp.zeros((chunk, 256), F32), jnp.zeros((chunk, 256), F32))
        top, bottom = lax.fori_loop(0, slots, plain, empty, unroll=4)
        estimate = top / (bottom + prior_weight)
        for _ in range(HUBER_ITERS):
            top, bottom = lax.fori_loop(
                0, slots, functools.partial(robust, estimate), empty, unroll=4
            )
            estimate = top / (bottom + prior_weight / huber_delta)
        field_ref[here, :] = estimate
        return carry

    lax.fori_loop(0, 64 // chunk, merge_rows, 0)
    exact = lax.Precision.HIGHEST
    ordered = jnp.dot(u_ref[...], field_ref[...], precision=exact, preferred_element_type=F32)
    for pair in range(2):
        here = slice(pair * 128, pair * 128 + 128)
        field_ref[:, here] = jnp.dot(
            ordered[:, here], v_ref[...], precision=exact, preferred_element_type=F32
        )


def order_matrices():
    q = np.zeros((128, 256), np.float32)
    u = np.zeros((64, 64), np.float32)
    v = np.zeros((128, 128), np.float32)
    for n in range(64):
        place = (n % 2) * 32 + n // 2
        q[n, place] = 1
        q[64 + n, 128 + place] = 1
        u[n, place] = 1
        v[place, n] = 1
        v[64 + place, 64 + n] = 1
    return jnp.asarray(q, BF), jnp.asarray(u), jnp.asarray(v)


MESH = pl.DeviceIdType.MESH


def exchange_kernel(
    quarters_ref,
    laid_ref,
    sent_ref,
    meta_ref,
    valid_ref,
    order_ref,
    w_in_raw,
    w_hid_raw,
    w_out_raw,
    q_ref,
    u_ref,
    v_ref,
    out_ref,
    planes_ref,
    codes_ref,
    weights_ref,
    matrices_ref,
    x_ref,
    own_ref,
    w_in_ref,
    w_hid_ref,
    stage_even,
    stage_odd,
    stage_code,
    y_ref,
    wt_ref,
    field_ref,
    near_left,
    near_right,
    last_ref,
    local_sems,
    x_send,
    x_recv,
    right_send,
    left_send,
    plane_recv,
    mat_send,
    mat_recv,
    code_send,
    code_recv,
    weight_send,
    weight_recv,
    mat_band_send,
    mat_band_recv,
    weight_band_send,
    weight_band_recv,
    twin_send,
    twin_recv,
    halo_send,
    halo_recv,
):
    tiles = planes_ref.shape[0]
    bands = quarters_ref.shape[0]
    scenes = laid_ref.shape[0]
    cap = sent_ref.shape[0] // tiles
    tile = lax.axis_index("tile")
    band = lax.axis_index("band")

    def tile_peer(k):
        return lax.rem(tile + k, tiles)

    def tile_source(k):
        return lax.rem(tile + tiles - k, tiles)

    def band_peer(k):
        return lax.rem(band + k, bands)

    def for_tiles(first, body):
        def step(k, carry):
            body(k)
            return carry

        lax.fori_loop(first, tiles, step, 0)

    barrier = pltpu.get_barrier_semaphore()
    for_tiles(
        1,
        lambda k: pl.semaphore_signal(
            barrier, inc=1, device_id={"tile": tile_peer(k)}, device_id_type=MESH
        ),
    )
    for k in range(1, bands):
        pl.semaphore_signal(barrier, inc=1, device_id={"band": band_peer(k)}, device_id_type=MESH)
    pl.semaphore_wait(barrier, tiles - 1 + bands - 1)

    def remote(src, dst, send, recv, where):
        return pltpu.make_async_remote_copy(
            src_ref=src,
            dst_ref=dst,
            send_sem=send,
            recv_sem=recv,
            device_id=where,
            device_id_type=MESH,
        )

    def x_copy(peer, source):
        return remote(
            quarters_ref.at[peer], x_ref.at[source], x_send.at[peer], x_recv.at[source],
            {"band": peer},
        )

    def plane_copy(shard, target, sems):
        return remote(
            planes_ref.at[shard], planes_ref.at[shard], sems.at[shard], plane_recv.at[shard],
            {"tile": target},
        )

    def own_plane_copy(target, sems):
        return remote(
            laid_ref, planes_ref.at[tile], sems.at[tile], plane_recv.at[tile], {"tile": target}
        )

    def mat_copy(peer, source):
        return remote(
            sent_ref.at[pl.ds(peer * cap, cap)], matrices_ref.at[band, source],
            mat_send.at[peer], mat_recv.at[source], {"tile": peer},
        )

    def code_copy(peer, source):
        return remote(
            meta_ref.at[peer], codes_ref.at[source], code_send.at[peer], code_recv.at[source],
            {"tile": peer},
        )

    parity = lax.rem(tile, 2)
    twin = tile + 1 - 2 * parity

    def weight_copy(peer, source):
        return remote(
            own_ref, weights_ref.at[band, parity, source // 2], weight_send.at[peer],
            weight_recv.at[source], {"tile": peer},
        )

    def mat_band_copy(source, peer, owner):
        return remote(
            matrices_ref.at[owner, source], matrices_ref.at[owner, source],
            mat_band_send.at[peer], mat_band_recv.at[owner], {"band": peer},
        )

    def weight_band_copy(source, peer, owner):
        shard = weights_ref.at[owner, parity, source // 2]
        return remote(
            shard, shard, weight_band_send.at[peer], weight_band_recv.at[owner], {"band": peer}
        )

    def twin_copy(owner, side):
        shard = weights_ref.at[owner, side]
        return remote(shard, shard, twin_send.at[owner], twin_recv.at[owner], {"tile": twin})

    for k in range(1, bands):
        x_copy(band_peer(k), band).start()
    x_local = pltpu.make_async_copy(quarters_ref.at[band], x_ref.at[band], local_sems.at[0])
    x_local.start()

    @pl.when(tile < tiles - 1)
    def _():
        own_plane_copy(tile + 1, right_send).start()

    @pl.when(tile > 0)
    def _():
        own_plane_copy(tile - 1, left_send).start()

    def first_sends(k):
        mat_copy(tile_peer(k), tile).start()
        code_copy(tile_peer(k), tile).start()

    for_tiles(1, first_sends)
    plane_local = pltpu.make_async_copy(laid_ref, planes_ref.at[tile], local_sems.at[1])
    plane_local.start()
    mat_local = pltpu.make_async_copy(
        sent_ref.at[pl.ds(tile * cap, cap)], matrices_ref.at[band, tile], local_sems.at[2]
    )
    mat_local.start()
    code_local = pltpu.make_async_copy(meta_ref.at[tile], codes_ref.at[tile], local_sems.at[3])
    code_local.start()

    def forward(s):
        left, right = tile - s, tile + s

        @pl.when((left >= 0) & (tile < tiles - 1))
        def _():
            plane_copy(left, tile, right_send).wait_recv()
            plane_copy(left, tile + 1, right_send).start()

        @pl.when((right < tiles) & (tile > 0))
        def _():
            plane_copy(right, tile, left_send).wait_recv()
            plane_copy(right, tile - 1, left_send).start()

    def network(scene, carry):
        def silu(t):
            return (t + t * jnp.tanh(t)).astype(BF)

        x = jnp.concatenate([x_ref[b, scene] for b in range(bands)], axis=0)
        hidden = silu(jnp.dot(w_in_ref[...], x, preferred_element_type=F32))
        for layer in range(w_hid_ref.shape[0]):
            hidden = silu(jnp.dot(w_hid_ref[layer], hidden, preferred_element_type=F32))
        w_out = jnp.broadcast_to(w_out_raw[...].astype(F32), (16, w_out_raw.shape[1]))
        logits = jnp.dot(w_out.astype(BF), hidden, preferred_element_type=F32)
        row = jax.nn.sigmoid(-logits[0:1])
        pieces = [row[:, i * 128 : (i + 1) * 128] for i in range(row.shape[1] // 128)]
        shape = (len(pieces), 128)
        line = lax.broadcasted_iota(jnp.int32, shape, 0)
        lane = lax.broadcasted_iota(jnp.int32, shape, 1)
        valid = jnp.zeros(shape, F32)
        side = 2 * len(pieces)
        for i in range(side):
            here = (line == i // 2) & (lane // 64 == i % 2)
            valid = jnp.where(here, valid_ref[scene, band * side + i].astype(F32), valid)
        order = jnp.full(shape, order_ref[scene], jnp.int32).astype(F32)
        recency = jnp.exp(1.4 * order / (scenes * tiles) - 0.7)
        own_ref[scene] = (jnp.concatenate(pieces, axis=0) * valid * recency).astype(BF)
        return carry

    def share_matrices():
        mat_local.wait()
        for k in range(1, bands):
            mat_band_copy(tile, band_peer(k), band).start()

        def share(k):
            source = tile_source(k)
            mat_copy(tile, source).wait_recv()
            for j in range(1, bands):
                mat_band_copy(source, band_peer(j), band).start()

        for_tiles(1, share)

    w_in_ref[...] = (w_in_raw[...].astype(F32) * 0.5).T.astype(BF)
    for layer in range(w_hid_raw.shape[0]):
        w_hid_ref[layer] = (w_hid_raw[layer].astype(F32) * 0.5).T.astype(BF)
    for k in range(1, bands):
        source = lax.rem(band + bands - k, bands)
        x_copy(source, source).wait_recv()
    x_local.wait()
    steps = 1
    for first, last in ((0, 3), (3, 7), (7, 13), (13, 16)):
        if steps < min(4, tiles):
            forward(steps)
            steps += 1
        if first == 7:
            share_matrices()
        lax.fori_loop(first * scenes // 16, last * scenes // 16, network, 0)

    weight_local = pltpu.make_async_copy(
        own_ref, weights_ref.at[band, parity, tile // 2], local_sems.at[4]
    )
    weight_local.start()

    def for_same(body):
        def step(k, carry):
            body(2 * k)
            return carry

        lax.fori_loop(1, tiles // 2, step, 0)

    for_same(lambda k: weight_copy(tile_peer(k), tile).start())
    weight_local.wait()
    for k in range(1, bands):
        weight_band_copy(tile, band_peer(k), band).start()

    def share_weights(k):
        source = tile_source(k)
        weight_copy(tile, source).wait_recv()
        for j in range(1, bands):
            weight_band_copy(source, band_peer(j), band).start()

    if steps < tiles:
        forward(steps)
        steps += 1
    for_same(share_weights)
    twin_copy(band, parity).start()
    if steps < tiles:
        forward(steps)
        steps += 1
    plane_local.wait()
    code_local.wait()
    for_tiles(1, lambda k: code_copy(tile, tile_source(k)).wait_recv())
    code_copies = pltpu.make_async_copy(codes_ref, stage_code, local_sems.at[4])
    code_copies.start()

    def mat_band_all(peer):
        whole = matrices_ref.at[peer]
        return remote(
            whole, whole, mat_band_send.at[peer], mat_band_recv.at[peer], {"band": peer}
        )

    def weight_band_all(peer, side):
        whole = weights_ref.at[peer, side]
        return remote(
            whole, whole, weight_band_send.at[peer], weight_band_recv.at[peer], {"band": peer}
        )

    for k in range(1, bands):
        peer = band_peer(bands - k)
        mat_band_all(peer).wait_recv()
        weight_band_all(peer, parity).wait_recv()
        twin_copy(peer, parity).start()
    for b in range(bands):
        twin_copy(b, 1 - parity).wait_recv()
    code_copies.wait()

    edge = (tile == 0) | (tile == tiles - 1)
    inner = jnp.minimum(tile, tiles - 1 - tile)
    outward = jnp.where(tile < tiles - 1 - tile, 1, -1)

    def nearest(n):
        near = ((n + 1) // 2) * (1 - 2 * lax.rem(n, 2))
        return tile + jnp.where(n <= 2 * inner, near, (n - inner) * outward)

    stages = (stage_even, stage_odd)

    def stage(n, odd):
        return pltpu.make_async_copy(
            planes_ref.at[nearest(n)], stages[odd], local_sems.at[5 + odd]
        )

    stage(0, 0).start()

    def reproject(first, last):
        def turn(m, carry):
            for odd in range(2):
                n = 2 * m + odd
                stage(n, odd).wait()

                @pl.when((n + 1 < tiles) & jnp.logical_not(edge))
                def _():
                    stage(n + 1, 1 - odd).start()

                for r in range(cap):
                    reproject_slot(
                        r, cap, nearest(n), stage_code, stages[odd], weights_ref, matrices_ref,
                        q_ref, y_ref, wt_ref,
                    )

                @pl.when((n + 1 < tiles) & edge)
                def _():
                    plane_copy(nearest(n + 1), tile, right_send).wait_recv()
                    stage(n + 1, 1 - odd).start()

            return carry

        lax.fori_loop(first, last, turn, 0)

    if tiles <= 8:
        reproject(0, tiles // 4)
        for_tiles(steps, forward)
        reproject(tiles // 4, tiles // 2)
    else:
        for_tiles(steps, forward)
        reproject(0, tiles // 2)

    robust_merge(y_ref, wt_ref, field_ref, u_ref, v_ref)

    def halo(target, landing, way):
        return remote(
            field_ref, landing, halo_send.at[way], halo_recv.at[way], {"tile": target}
        )

    @pl.when(tile < tiles - 1)
    def _():
        halo(tile + 1, near_left, 0).start()

    @pl.when(tile > 0)
    def _():
        halo(tile - 1, near_right, 1).start()

    @pl.when(tile == 0)
    def _():
        near_left[...] = jnp.zeros_like(near_left)

    @pl.when(tile == tiles - 1)
    def _():
        near_right[...] = jnp.zeros_like(near_right)

    @pl.when(tile > 0)
    def _():
        halo(tile, near_left, 0).wait_recv()

    @pl.when(tile < tiles - 1)
    def _():
        halo(tile, near_right, 1).wait_recv()

    lane = lax.broadcasted_iota(jnp.int32, (64, 128), 1)
    line = lax.broadcasted_iota(jnp.int32, (64, 128), 0)
    shut = ((lane == 127) & (tile == 0)) | ((lane == 63) & (tile == tiles - 1))
    for c in range(out_ref.shape[0]):
        pair = pl.ds((c // 2) * 128, 128)
        own, low, high = field_ref[:, pair], near_left[:, pair], near_right[:, pair]
        if c % 2 == 0:
            low, high = pltpu.roll(low, 64, 1), pltpu.roll(high, 64, 1)
        else:
            own = pltpu.roll(own, 64, 1)
        g = jnp.where(lane < 64, own, jnp.where(lane < 96, high, low))
        for _ in range(SMOOTH):
            across = pltpu.roll(g, 127, 1) - g
            side = jnp.where(shut, 0.0, across / (1.0 + across * across))
            down = pltpu.roll(g, 63, 0) - g
            upright = jnp.where(line == 63, 0.0, down / (1.0 + down * down))
            g = g + smooth_rate * (
                side - pltpu.roll(side, 1, 1) + (upright - pltpu.roll(upright, 1, 0))
            )
        last_ref[c] = g
        even = last_ref[c, pl.ds(0, 32, stride=2), :]
        odd = last_ref[c, pl.ds(1, 32, stride=2), :]
        out_ref[c] = jnp.where(lane[:32] < 64, even, pltpu.roll(odd, 64, 1))

    @pl.when(tile < tiles - 1)
    def _():
        halo(tile + 1, near_left, 0).wait_send()

    @pl.when(tile > 0)
    def _():
        halo(tile - 1, near_right, 1).wait_send()

    def finish(k):
        code_copy(tile_peer(k), tile).wait_send()
        mat_copy(tile_peer(k), tile).wait_send()

    for_tiles(1, finish)
    for_same(lambda k: weight_copy(tile_peer(k), tile).wait_send())

    def finish_planes(shard):
        @pl.when((shard <= tile) & (tile < tiles - 1))
        def _():
            plane_copy(shard, tile, right_send).wait_send()

        @pl.when((shard >= tile) & (tile > 0))
        def _():
            plane_copy(shard, tile, left_send).wait_send()

    for_tiles(0, finish_planes)
    for k in range(1, bands):
        peer = band_peer(k)
        x_copy(peer, band).wait_send()
        mat_band_all(peer).wait_send()
        weight_band_all(peer, parity).wait_send()
    for b in range(bands):
        twin_copy(b, parity).wait_send()


def exchange(quarters, laid, sent, meta, valid_rows, scene_order, w_in, w_hidden, w_out):
    bands, scenes, part, width = quarters.shape
    tiles = meta.shape[0]
    cap = sent.shape[0] // tiles
    hid = w_in.shape[1]
    layers = w_hidden.shape[0]
    lines = width // 128
    anywhere = pl.BlockSpec(memory_space=pl.ANY)
    vmem = pl.BlockSpec(memory_space=pltpu.VMEM)
    smem = pl.BlockSpec(memory_space=pltpu.SMEM)
    dma = pltpu.SemaphoreType.DMA
    return pl.pallas_call(
        exchange_kernel,
        in_specs=[anywhere] * 4 + [smem] * 2 + [vmem] * 6,
        out_specs=[vmem] + [anywhere] * 2,
        out_shape=[
            jax.ShapeDtypeStruct(laid.shape[1:], F32),
            jax.ShapeDtypeStruct((tiles,) + laid.shape, BF),
            jax.ShapeDtypeStruct(meta.shape, jnp.int32),
        ],
        scratch_shapes=[
            pltpu.VMEM((bands, 2, tiles // 2, scenes, lines, 128), BF),
            pltpu.VMEM((bands, tiles, cap) + sent.shape[1:], BF),
            pltpu.VMEM(quarters.shape, BF),
            pltpu.VMEM((scenes, lines, 128), BF),
            pltpu.VMEM((hid, bands * part), BF),
            pltpu.VMEM((layers, hid, hid), BF),
            pltpu.VMEM(laid.shape, BF),
            pltpu.VMEM(laid.shape, BF),
            pltpu.SMEM(meta.shape, jnp.int32),
            pltpu.VMEM((tiles * cap, 64, 256), F32),
            pltpu.VMEM((tiles * cap, 64, 128), F32),
            pltpu.VMEM((64, 256), F32),
            pltpu.VMEM((64, 256), F32),
            pltpu.VMEM((64, 256), F32),
            pltpu.VMEM((part, 64, 128), F32),
            dma((7,)),
            dma((bands,)),
            dma((bands,)),
        ]
        + [dma((tiles,))] * 9
        + [dma((bands,))] * 6
        + [dma((2,))] * 2,
        compiler_params=pltpu.CompilerParams(
            collective_id=0, has_side_effects=True, vmem_limit_bytes=40 * 1024 * 1024
        ),
    )(
        quarters, laid, sent, meta, valid_rows, scene_order, w_in, w_hidden, w_out[None, :],
        *order_matrices(),
    )[0]


def per_device(
    granules,
    valid_rows,
    scene_order,
    intersections,
    row_resample,
    col_resample,
    w_in,
    w_hidden,
    w_out,
):
    scenes, group_bands, pixel_count = granules.shape
    top = intersections.shape[1]
    tile_count = lax.axis_size("tile")
    band_count = lax.axis_size("band")
    band = lax.axis_index("band")
    tile = lax.axis_index("tile")
    entry_count = scenes * top
    cap = (entry_count + tile_count - 1) // tile_count + 1
    part = pixel_count // band_count

    laid = granules.reshape(scenes, group_bands, pixel_count // 128, 128)
    quarters = jnp.stack([granules[:, :, b * part : (b + 1) * part] for b in range(band_count)])
    flat_dest = intersections.reshape(entry_count)
    is_dest = flat_dest[None, :] == jnp.arange(tile_count, dtype=jnp.int32)[:, None]
    rank = jnp.cumsum(is_dest.astype(jnp.int32), 1) - 1
    pick = is_dest[:, None, :] & (rank[:, None, :] == jnp.arange(cap)[None, :, None])
    scene_ids = (jnp.arange(entry_count, dtype=jnp.int32) // top + 1)[None, None, :]
    code = jnp.sum(jnp.where(pick, scene_ids, 0), 2) - 1
    meta = jnp.zeros((tile_count, 8, 128), jnp.int32).at[:, 0, :cap].set(code)
    pick = pick.reshape(tile_count * cap, entry_count).astype(BF)
    both = jnp.concatenate(
        [
            lax.dynamic_slice_in_dim(m, band * part, part, 2).reshape(entry_count, part)
            for m in (row_resample, col_resample)
        ],
        1,
    )
    sent = jnp.dot(pick, both, preferred_element_type=F32).astype(BF)
    sent = sent.reshape(tile_count * cap, 2 * part // 128, 128)
    field = exchange(
        quarters, laid, sent, meta, valid_rows, scene_order, w_in, w_hidden, w_out
    )
    return field.reshape(group_bands, pixel_count)


def solution(mesh):
    return jax.shard_map(
        per_device,
        mesh=mesh,
        in_specs=(
            P("tile", "band", None),
            P("tile", None),
            P("tile"),
            P("tile", None),
            P("tile", None, None),
            P("tile", None, None),
            P(),
            P(),
            P(),
        ),
        out_specs=P("band", "tile"),
        check_vma=False,
    )
```

```python
import functools

import jax
import jax.numpy as jnp
import numpy as np
from jax import lax
from jax.experimental import pallas as pl
from jax.experimental.pallas import tpu as pltpu
from jax.sharding import PartitionSpec as P

HUBER_ITERS = 4
SMOOTH = 2
prior_weight = 0.25
huber_delta = 0.5
smooth_rate = 0.2
BF = jnp.bfloat16
F32 = jnp.float32


def reproject_slot(r, cap, source, code_ref, x_ref, w_ref, m_ref, q_ref, y_ref, wt_ref):
    slot = source * cap + r
    side, place = lax.rem(source, 2), source // 2
    lane = lax.broadcasted_iota(jnp.int32, (32, 128), 1)
    low = lane < 64
    quarters = range(m_ref.shape[0])
    code = code_ref[source, 0, r]
    scene = jnp.maximum(code, 0)
    present = jnp.minimum(code + 1, 1).astype(F32)
    planes = x_ref[scene]
    weight = jnp.concatenate([w_ref[b, side, place, scene] for b in quarters], axis=0)
    rows = jnp.concatenate([m_ref[b, source, r, 0:8] for b in quarters], axis=0)
    cols = jnp.concatenate([m_ref[b, source, r, 8:16] for b in quarters], axis=0).astype(F32)
    turned = pltpu.roll(cols, 64, 1)
    zero = jnp.zeros((32, 128), F32)
    first = jnp.concatenate([jnp.where(low, cols, zero), jnp.where(low, turned, zero)], 0)
    second = jnp.concatenate([jnp.where(low, zero, turned), jnp.where(low, zero, cols)], 0)
    first, second = first.astype(BF), second.astype(BF)
    blank = jnp.zeros((64, 128), BF)
    right = jnp.concatenate(
        [
            jnp.concatenate([first, blank], 1),
            jnp.concatenate([blank, first], 1),
            jnp.concatenate([second, blank], 1),
            jnp.concatenate([blank, second], 1),
        ],
        0,
    )
    left = jnp.concatenate(
        [
            jnp.concatenate([planes[0], planes[1]], 1),
            jnp.concatenate([planes[2], planes[3]], 1),
            jnp.concatenate([weight, weight], 1),
        ],
        0,
    )
    half = lax.dot_general(
        left, right, (((1,), (1,)), ((), ())), preferred_element_type=F32
    ).astype(BF)
    stacked = jnp.concatenate(
        [
            jnp.concatenate([half[p * 32 : p * 32 + 32, 0:128] for p in range(3)], 1),
            jnp.concatenate([half[p * 32 : p * 32 + 32, 128:256] for p in range(3)], 1),
        ],
        0,
    )
    spread = jnp.dot(rows, q_ref[...], preferred_element_type=F32).astype(BF)
    row_matrix = jnp.concatenate([spread[:, 0:64], spread[:, 128:192]], 0)
    moved = jnp.dot(row_matrix, stacked, preferred_element_type=F32).astype(BF).astype(F32)
    y_ref[slot] = moved[:, 0:256]
    wt_ref[slot] = moved[:, 256:384] * present


def robust_merge(y_ref, wt_ref, field_ref, u_ref, v_ref):
    slots = y_ref.shape[0]
    chunk = 16

    def merge_rows(i, carry):
        here = pl.ds(pl.multiple_of(i * chunk, chunk), chunk)

        def load(n):
            w = wt_ref[n, here, :]
            return y_ref[n, here, :], jnp.concatenate([w, w], 1)

        def plain(n, sums):
            y, w = load(n)
            return sums[0] + w * y, sums[1] + w

        def robust(estimate, n, sums):
            y, w = load(n)
            size = jnp.maximum(jnp.abs(y - estimate), huber_delta)
            h = w * pl.reciprocal(size, approx=True)
            return sums[0] + h * y, sums[1] + h

        empty = (jnp.zeros((chunk, 256), F32), jnp.zeros((chunk, 256), F32))
        top, bottom = lax.fori_loop(0, slots, plain, empty, unroll=8)
        estimate = top / (bottom + prior_weight)
        for _ in range(HUBER_ITERS):
            top, bottom = lax.fori_loop(
                0, slots, functools.partial(robust, estimate), empty, unroll=8
            )
            estimate = top / (bottom + prior_weight / huber_delta)
        field_ref[here, :] = estimate
        return carry

    lax.fori_loop(0, 64 // chunk, merge_rows, 0)
    exact = lax.Precision.HIGHEST
    ordered = jnp.dot(u_ref[...], field_ref[...], precision=exact, preferred_element_type=F32)
    for pair in range(2):
        here = slice(pair * 128, pair * 128 + 128)
        field_ref[:, here] = jnp.dot(
            ordered[:, here], v_ref[...], precision=exact, preferred_element_type=F32
        )


def order_matrices():
    q = np.zeros((128, 256), np.float32)
    u = np.zeros((64, 64), np.float32)
    v = np.zeros((128, 128), np.float32)
    for n in range(64):
        place = (n % 2) * 32 + n // 2
        q[n, place] = 1
        q[64 + n, 128 + place] = 1
        u[n, place] = 1
        v[place, n] = 1
        v[64 + place, 64 + n] = 1
    return jnp.asarray(q, BF), jnp.asarray(u), jnp.asarray(v)


MESH = pl.DeviceIdType.MESH


def exchange_kernel(
    granules_ref,
    laid_ref,
    sent_ref,
    meta_ref,
    valid_ref,
    order_ref,
    w_in_raw,
    w_hid_raw,
    w_out_raw,
    q_ref,
    u_ref,
    v_ref,
    out_ref,
    planes_ref,
    codes_ref,
    weights_ref,
    matrices_ref,
    x_ref,
    own_ref,
    w_in_ref,
    w_hid_ref,
    stage_even,
    stage_odd,
    stage_code,
    y_ref,
    wt_ref,
    field_ref,
    near_left,
    near_right,
    last_ref,
    local_sems,
    x_send,
    x_recv,
    right_send,
    left_send,
    plane_recv,
    mat_send,
    mat_recv,
    code_send,
    code_recv,
    weight_send,
    weight_recv,
    mat_band_send,
    mat_band_recv,
    weight_band_send,
    weight_band_recv,
    twin_send,
    twin_recv,
    halo_send,
    halo_recv,
):
    tiles = planes_ref.shape[0]
    bands = x_ref.shape[0]
    scenes = laid_ref.shape[0]
    cap = sent_ref.shape[0] // tiles
    tile = lax.axis_index("tile")
    band = lax.axis_index("band")

    def tile_peer(k):
        return lax.rem(tile + k, tiles)

    def tile_source(k):
        return lax.rem(tile + tiles - k, tiles)

    def band_peer(k):
        return lax.rem(band + k, bands)

    def for_tiles(first, body):
        def step(k, carry):
            body(k)
            return carry

        lax.fori_loop(first, tiles, step, 0)

    edge = (tile == 0) | (tile == tiles - 1)
    inner = jnp.minimum(tile, tiles - 1 - tile)
    outward = jnp.where(tile < tiles - 1 - tile, 1, -1)

    def nearest(n):
        near = ((n + 1) // 2) * (1 - 2 * lax.rem(n, 2))
        return tile + jnp.where(n <= 2 * inner, near, (n - inner) * outward)

    barrier = pltpu.get_barrier_semaphore()
    for_tiles(
        1,
        lambda k: pl.semaphore_signal(
            barrier, inc=1, device_id={"tile": tile_peer(k)}, device_id_type=MESH
        ),
    )
    for k in range(1, bands):
        pl.semaphore_signal(barrier, inc=1, device_id={"band": band_peer(k)}, device_id_type=MESH)
    pl.semaphore_wait(barrier, tiles - 1 + bands - 1)

    def remote(src, dst, send, recv, where):
        return pltpu.make_async_remote_copy(
            src_ref=src,
            dst_ref=dst,
            send_sem=send,
            recv_sem=recv,
            device_id=where,
            device_id_type=MESH,
        )

    width = x_ref.shape[3]

    def quarter(b):
        return granules_ref.at[:, :, pl.ds(pl.multiple_of(b * width, width), width)]

    def x_copy(peer, source):
        return remote(
            quarter(peer), x_ref.at[source], x_send.at[peer], x_recv.at[source],
            {"band": peer},
        )

    def plane_copy(shard, target, sems):
        return remote(
            planes_ref.at[shard], planes_ref.at[shard], sems.at[shard], plane_recv.at[shard],
            {"tile": target},
        )

    def own_plane_copy(target, sems):
        return remote(
            laid_ref, planes_ref.at[tile], sems.at[tile], plane_recv.at[tile], {"tile": target}
        )

    def mat_copy(peer, source):
        return remote(
            sent_ref.at[pl.ds(peer * cap, cap)], matrices_ref.at[band, source],
            mat_send.at[peer], mat_recv.at[source], {"tile": peer},
        )

    def code_copy(peer, source):
        return remote(
            meta_ref.at[peer], codes_ref.at[source], code_send.at[peer], code_recv.at[source],
            {"tile": peer},
        )

    parity = lax.rem(tile, 2)
    twin = tile + 1 - 2 * parity

    def weight_copy(peer, source):
        return remote(
            own_ref, weights_ref.at[band, parity, source // 2], weight_send.at[peer],
            weight_recv.at[source], {"tile": peer},
        )

    def mat_band_copy(source, peer, owner):
        return remote(
            matrices_ref.at[owner, source], matrices_ref.at[owner, source],
            mat_band_send.at[peer], mat_band_recv.at[owner], {"band": peer},
        )

    def weight_band_copy(source, peer, owner):
        shard = weights_ref.at[owner, parity, source // 2]
        return remote(
            shard, shard, weight_band_send.at[peer], weight_band_recv.at[owner], {"band": peer}
        )

    def twin_copy(owner, side):
        shard = weights_ref.at[owner, side]
        return remote(shard, shard, twin_send.at[owner], twin_recv.at[owner], {"tile": twin})

    for k in range(1, bands):
        x_copy(band_peer(k), band).start()
    x_local = pltpu.make_async_copy(quarter(band), x_ref.at[band], local_sems.at[0])
    x_local.start()

    @pl.when(tile < tiles - 1)
    def _():
        own_plane_copy(tile + 1, right_send).start()

    @pl.when(tile > 0)
    def _():
        own_plane_copy(tile - 1, left_send).start()

    def first_sends(k):
        mat_copy(tile_peer(k), tile).start()
        code_copy(tile_peer(k), tile).start()

    for_tiles(1, first_sends)
    plane_local = pltpu.make_async_copy(laid_ref, planes_ref.at[tile], local_sems.at[1])
    plane_local.start()
    mat_local = pltpu.make_async_copy(
        sent_ref.at[pl.ds(tile * cap, cap)], matrices_ref.at[band, tile], local_sems.at[2]
    )
    mat_local.start()
    code_local = pltpu.make_async_copy(meta_ref.at[tile], codes_ref.at[tile], local_sems.at[3])
    code_local.start()

    def forward(s):
        left, right = tile - s, tile + s

        @pl.when((left >= 0) & (tile < tiles - 1))
        def _():
            plane_copy(left, tile, right_send).wait_recv()
            plane_copy(left, tile + 1, right_send).start()

        @pl.when((right < tiles) & (tile > 0))
        def _():
            plane_copy(right, tile, left_send).wait_recv()
            plane_copy(right, tile - 1, left_send).start()

    def network(scene, carry):
        def silu(t):
            return (t + t * jnp.tanh(t)).astype(BF)

        x = jnp.concatenate([x_ref[b, scene] for b in range(bands)], axis=0)
        hidden = silu(jnp.dot(w_in_ref[...], x, preferred_element_type=F32))
        for layer in range(w_hid_ref.shape[0]):
            hidden = silu(jnp.dot(w_hid_ref[layer], hidden, preferred_element_type=F32))
        w_out = jnp.broadcast_to(w_out_raw[...].astype(F32), (16, w_out_raw.shape[1]))
        logits = jnp.dot(w_out.astype(BF), hidden, preferred_element_type=F32)
        row = jax.nn.sigmoid(-logits[0:1])
        pieces = [row[:, i * 128 : (i + 1) * 128] for i in range(row.shape[1] // 128)]
        shape = (len(pieces), 128)
        line = lax.broadcasted_iota(jnp.int32, shape, 0)
        lane = lax.broadcasted_iota(jnp.int32, shape, 1)
        valid = jnp.zeros(shape, F32)
        side = 2 * len(pieces)
        for i in range(side):
            here = (line == i // 2) & (lane // 64 == i % 2)
            valid = jnp.where(here, valid_ref[scene, band * side + i].astype(F32), valid)
        order = jnp.full(shape, order_ref[scene], jnp.int32).astype(F32)
        recency = jnp.exp(1.4 * order / (scenes * tiles) - 0.7)
        own_ref[scene] = (jnp.concatenate(pieces, axis=0) * valid * recency).astype(BF)
        return carry

    def share_matrices(first, last):
        def share(n, carry):
            source = nearest(n)
            mat_copy(tile, source).wait_recv()
            for j in range(1, bands):
                mat_band_copy(source, band_peer(j), band).start()
            return carry

        lax.fori_loop(first, last, share, 0)

    w_in_ref[...] = (w_in_raw[...].astype(F32) * 0.5).T.astype(BF)
    for layer in range(w_hid_raw.shape[0]):
        w_hid_ref[layer] = (w_hid_raw[layer].astype(F32) * 0.5).T.astype(BF)
    for k in range(1, bands):
        source = lax.rem(band + bands - k, bands)
        x_copy(source, source).wait_recv()
    x_local.wait()
    steps = 1
    for part in range(4):
        if steps < min(4, tiles):
            forward(steps)
            steps += 1
        if part == 2:
            mat_local.wait()
            for k in range(1, bands):
                mat_band_copy(tile, band_peer(k), band).start()
            share_matrices(1, tiles // 2)
        lax.fori_loop(part * scenes // 4, (part + 1) * scenes // 4, network, 0, unroll=2)

    weight_local = pltpu.make_async_copy(
        own_ref, weights_ref.at[band, parity, tile // 2], local_sems.at[4]
    )
    weight_local.start()

    def for_same(body):
        def step(k, carry):
            body(2 * k)
            return carry

        lax.fori_loop(1, tiles // 2, step, 0)

    for_same(lambda k: weight_copy(tile_peer(k), tile).start())
    weight_local.wait()
    for k in range(1, bands):
        weight_band_copy(tile, band_peer(k), band).start()

    def share_weights(n):
        source = nearest(n)

        @pl.when(lax.rem(source + tile, 2) == 0)
        def _():
            weight_copy(tile, source).wait_recv()
            for j in range(1, bands):
                weight_band_copy(source, band_peer(j), band).start()

    share_matrices(tiles // 2, tiles)
    for_tiles(1, share_weights)
    twin_copy(band, parity).start()
    if steps < tiles:
        forward(steps)
        steps += 1
    plane_local.wait()
    code_local.wait()
    for_tiles(1, lambda k: code_copy(tile, tile_source(k)).wait_recv())
    code_copies = pltpu.make_async_copy(codes_ref, stage_code, local_sems.at[4])
    code_copies.start()

    def mat_band_all(peer):
        whole = matrices_ref.at[peer]
        return remote(
            whole, whole, mat_band_send.at[peer], mat_band_recv.at[peer], {"band": peer}
        )

    def weight_band_all(peer, side):
        whole = weights_ref.at[peer, side]
        return remote(
            whole, whole, weight_band_send.at[peer], weight_band_recv.at[peer], {"band": peer}
        )

    for k in range(1, bands):
        peer = band_peer(bands - k)
        mat_band_all(peer).wait_recv()
        weight_band_all(peer, parity).wait_recv()
        twin_copy(peer, parity).start()
    for b in range(bands):
        twin_copy(b, 1 - parity).wait_recv()
    code_copies.wait()

    stages = (stage_even, stage_odd)

    def stage(n, odd):
        return pltpu.make_async_copy(
            planes_ref.at[nearest(n)], stages[odd], local_sems.at[5 + odd]
        )

    stage(0, 0).start()

    def reproject(first, last):
        def turn(m, carry):
            for odd in range(2):
                n = 2 * m + odd
                stage(n, odd).wait()

                @pl.when((n + 1 < tiles) & jnp.logical_not(edge))
                def _():
                    stage(n + 1, 1 - odd).start()

                for r in range(cap):
                    reproject_slot(
                        r, cap, nearest(n), stage_code, stages[odd], weights_ref, matrices_ref,
                        q_ref, y_ref, wt_ref,
                    )

                @pl.when((n + 1 < tiles) & edge)
                def _():
                    plane_copy(nearest(n + 1), tile, right_send).wait_recv()
                    stage(n + 1, 1 - odd).start()

            return carry

        lax.fori_loop(first, last, turn, 0)

    if tiles <= 8:
        reproject(0, tiles // 4)
        for_tiles(steps, forward)
        reproject(tiles // 4, tiles // 2)
    else:
        for_tiles(steps, forward)
        reproject(0, tiles // 2)

    robust_merge(y_ref, wt_ref, field_ref, u_ref, v_ref)

    def halo(target, landing, way):
        return remote(
            field_ref, landing, halo_send.at[way], halo_recv.at[way], {"tile": target}
        )

    @pl.when(tile < tiles - 1)
    def _():
        halo(tile + 1, near_left, 0).start()

    @pl.when(tile > 0)
    def _():
        halo(tile - 1, near_right, 1).start()

    @pl.when(tile == 0)
    def _():
        near_left[...] = jnp.zeros_like(near_left)

    @pl.when(tile == tiles - 1)
    def _():
        near_right[...] = jnp.zeros_like(near_right)

    @pl.when(tile > 0)
    def _():
        halo(tile, near_left, 0).wait_recv()

    @pl.when(tile < tiles - 1)
    def _():
        halo(tile, near_right, 1).wait_recv()

    lane = lax.broadcasted_iota(jnp.int32, (64, 128), 1)
    line = lax.broadcasted_iota(jnp.int32, (64, 128), 0)
    shut = ((lane == 127) & (tile == 0)) | ((lane == 63) & (tile == tiles - 1))
    for c in range(out_ref.shape[0]):
        pair = pl.ds((c // 2) * 128, 128)
        own, low, high = field_ref[:, pair], near_left[:, pair], near_right[:, pair]
        if c % 2 == 0:
            low, high = pltpu.roll(low, 64, 1), pltpu.roll(high, 64, 1)
        else:
            own = pltpu.roll(own, 64, 1)
        g = jnp.where(lane < 64, own, jnp.where(lane < 96, high, low))
        for _ in range(SMOOTH):
            across = pltpu.roll(g, 127, 1) - g
            side = jnp.where(shut, 0.0, across / (1.0 + across * across))
            down = pltpu.roll(g, 63, 0) - g
            upright = jnp.where(line == 63, 0.0, down / (1.0 + down * down))
            g = g + smooth_rate * (
                side - pltpu.roll(side, 1, 1) + (upright - pltpu.roll(upright, 1, 0))
            )
        last_ref[c] = g
        even = last_ref[c, pl.ds(0, 32, stride=2), :]
        odd = last_ref[c, pl.ds(1, 32, stride=2), :]
        out_ref[c] = jnp.where(lane[:32] < 64, even, pltpu.roll(odd, 64, 1))

    @pl.when(tile < tiles - 1)
    def _():
        halo(tile + 1, near_left, 0).wait_send()

    @pl.when(tile > 0)
    def _():
        halo(tile - 1, near_right, 1).wait_send()

    def finish(k):
        code_copy(tile_peer(k), tile).wait_send()
        mat_copy(tile_peer(k), tile).wait_send()

    for_tiles(1, finish)
    for_same(lambda k: weight_copy(tile_peer(k), tile).wait_send())

    def finish_planes(shard):
        @pl.when((shard <= tile) & (tile < tiles - 1))
        def _():
            plane_copy(shard, tile, right_send).wait_send()

        @pl.when((shard >= tile) & (tile > 0))
        def _():
            plane_copy(shard, tile, left_send).wait_send()

    for_tiles(0, finish_planes)
    for k in range(1, bands):
        peer = band_peer(k)
        x_copy(peer, band).wait_send()
        mat_band_all(peer).wait_send()
        weight_band_all(peer, parity).wait_send()
    for b in range(bands):
        twin_copy(b, parity).wait_send()


def exchange(granules, bands, laid, sent, meta, valid_rows, scene_order, w_in, w_hidden, w_out):
    scenes, part, pixels = granules.shape
    width = pixels // bands
    tiles = meta.shape[0]
    cap = sent.shape[0] // tiles
    hid = w_in.shape[1]
    layers = w_hidden.shape[0]
    lines = width // 128
    anywhere = pl.BlockSpec(memory_space=pl.ANY)
    vmem = pl.BlockSpec(memory_space=pltpu.VMEM)
    smem = pl.BlockSpec(memory_space=pltpu.SMEM)
    dma = pltpu.SemaphoreType.DMA
    return pl.pallas_call(
        exchange_kernel,
        in_specs=[anywhere] * 4 + [smem] * 2 + [vmem] * 6,
        out_specs=[vmem] + [anywhere] * 2,
        out_shape=[
            jax.ShapeDtypeStruct(laid.shape[1:], F32),
            jax.ShapeDtypeStruct((tiles,) + laid.shape, BF),
            jax.ShapeDtypeStruct(meta.shape, jnp.int32),
        ],
        scratch_shapes=[
            pltpu.VMEM((bands, 2, tiles // 2, scenes, lines, 128), BF),
            pltpu.VMEM((bands, tiles, cap) + sent.shape[1:], BF),
            pltpu.VMEM((bands, scenes, part, width), BF),
            pltpu.VMEM((scenes, lines, 128), BF),
            pltpu.VMEM((hid, bands * part), BF),
            pltpu.VMEM((layers, hid, hid), BF),
            pltpu.VMEM(laid.shape, BF),
            pltpu.VMEM(laid.shape, BF),
            pltpu.SMEM(meta.shape, jnp.int32),
            pltpu.VMEM((tiles * cap, 64, 256), F32),
            pltpu.VMEM((tiles * cap, 64, 128), F32),
            pltpu.VMEM((64, 256), F32),
            pltpu.VMEM((64, 256), F32),
            pltpu.VMEM((64, 256), F32),
            pltpu.VMEM((part, 64, 128), F32),
            dma((7,)),
            dma((bands,)),
            dma((bands,)),
        ]
        + [dma((tiles,))] * 9
        + [dma((bands,))] * 6
        + [dma((2,))] * 2,
        compiler_params=pltpu.CompilerParams(
            collective_id=0, has_side_effects=True, vmem_limit_bytes=40 * 1024 * 1024
        ),
    )(
        granules, laid, sent, meta, valid_rows, scene_order, w_in, w_hidden, w_out[None, :],
        *order_matrices(),
    )[0]


def per_device(
    granules,
    valid_rows,
    scene_order,
    intersections,
    row_resample,
    col_resample,
    w_in,
    w_hidden,
    w_out,
):
    scenes, group_bands, pixel_count = granules.shape
    top = intersections.shape[1]
    tile_count = lax.axis_size("tile")
    band_count = lax.axis_size("band")
    band = lax.axis_index("band")
    tile = lax.axis_index("tile")
    entry_count = scenes * top
    cap = (entry_count + tile_count - 1) // tile_count + 1
    part = pixel_count // band_count

    laid = granules.reshape(scenes, group_bands, pixel_count // 128, 128)
    flat_dest = intersections.reshape(entry_count)
    is_dest = flat_dest[None, :] == jnp.arange(tile_count, dtype=jnp.int32)[:, None]
    rank = jnp.cumsum(is_dest.astype(jnp.int32), 1) - 1
    pick = is_dest[:, None, :] & (rank[:, None, :] == jnp.arange(cap)[None, :, None])
    scene_ids = (jnp.arange(entry_count, dtype=jnp.int32) // top + 1)[None, None, :]
    code = jnp.sum(jnp.where(pick, scene_ids, 0), 2) - 1
    meta = jnp.zeros((tile_count, 8, 128), jnp.int32).at[:, 0, :cap].set(code)
    pick = pick.reshape(tile_count * cap, entry_count).astype(BF)
    both = jnp.concatenate(
        [
            lax.dynamic_slice_in_dim(m, band * part, part, 2).reshape(entry_count, part)
            for m in (row_resample, col_resample)
        ],
        1,
    )
    sent = jnp.dot(pick, both, preferred_element_type=F32).astype(BF)
    sent = sent.reshape(tile_count * cap, 2 * part // 128, 128)
    field = exchange(
        granules, band_count, laid, sent, meta, valid_rows, scene_order, w_in, w_hidden, w_out
    )
    return field.reshape(group_bands, pixel_count)


def solution(mesh):
    return jax.shard_map(
        per_device,
        mesh=mesh,
        in_specs=(
            P("tile", "band", None),
            P("tile", None),
            P("tile"),
            P("tile", None),
            P("tile", None, None),
            P("tile", None, None),
            P(),
            P(),
            P(),
        ),
        out_specs=P("band", "tile"),
        check_vma=False,
    )
```

```python
import functools

import jax
import jax.numpy as jnp
import numpy as np
from jax import lax
from jax.experimental import pallas as pl
from jax.experimental.pallas import tpu as pltpu
from jax.sharding import PartitionSpec as P

HUBER_ITERS = 4
SMOOTH = 2
prior_weight = 0.25
huber_delta = 0.5
smooth_rate = 0.2
BF = jnp.bfloat16
F32 = jnp.float32


def reproject_slot(r, cap, source, code_ref, x_ref, w_ref, m_ref, q_ref, y_ref, wt_ref):
    slot = source * cap + r
    side, place = lax.rem(source, 2), source // 2
    lane = lax.broadcasted_iota(jnp.int32, (32, 128), 1)
    low = lane < 64
    quarters = range(m_ref.shape[0])
    code = code_ref[source, 0, r]
    scene = jnp.maximum(code, 0)
    present = jnp.minimum(code + 1, 1).astype(F32)
    planes = x_ref[scene]
    weight = jnp.concatenate([w_ref[b, side, place, scene] for b in quarters], axis=0)
    rows = jnp.concatenate([m_ref[b, source, r, 0:8] for b in quarters], axis=0)
    cols = jnp.concatenate([m_ref[b, source, r, 8:16] for b in quarters], axis=0).astype(F32)
    turned = pltpu.roll(cols, 64, 1)
    zero = jnp.zeros((32, 128), F32)
    first = jnp.concatenate([jnp.where(low, cols, zero), jnp.where(low, turned, zero)], 0)
    second = jnp.concatenate([jnp.where(low, zero, turned), jnp.where(low, zero, cols)], 0)
    first, second = first.astype(BF), second.astype(BF)
    blank = jnp.zeros((64, 128), BF)
    right = jnp.concatenate(
        [
            jnp.concatenate([first, blank], 1),
            jnp.concatenate([blank, first], 1),
            jnp.concatenate([second, blank], 1),
            jnp.concatenate([blank, second], 1),
        ],
        0,
    )
    left = jnp.concatenate(
        [
            jnp.concatenate([planes[0], planes[1]], 1),
            jnp.concatenate([planes[2], planes[3]], 1),
            jnp.concatenate([weight, weight], 1),
        ],
        0,
    )
    half = lax.dot_general(
        left, right, (((1,), (1,)), ((), ())), preferred_element_type=F32
    ).astype(BF)
    stacked = jnp.concatenate(
        [
            jnp.concatenate([half[p * 32 : p * 32 + 32, 0:128] for p in range(3)], 1),
            jnp.concatenate([half[p * 32 : p * 32 + 32, 128:256] for p in range(3)], 1),
        ],
        0,
    )
    spread = jnp.dot(rows, q_ref[...], preferred_element_type=F32).astype(BF)
    row_matrix = jnp.concatenate([spread[:, 0:64], spread[:, 128:192]], 0)
    moved = jnp.dot(row_matrix, stacked, preferred_element_type=F32).astype(BF).astype(F32)
    y_ref[slot] = moved[:, 0:256]
    wt_ref[slot] = moved[:, 256:384] * present


def robust_merge(y_ref, wt_ref, field_ref, u_ref, v_ref):
    slots = y_ref.shape[0]
    chunk = 16

    def merge_rows(i, carry):
        here = pl.ds(pl.multiple_of(i * chunk, chunk), chunk)

        def load(n):
            w = wt_ref[n, here, :]
            return y_ref[n, here, :], jnp.concatenate([w, w], 1)

        def plain(n, sums):
            y, w = load(n)
            return sums[0] + w * y, sums[1] + w

        def robust(estimate, n, sums):
            y, w = load(n)
            size = jnp.maximum(jnp.abs(y - estimate), huber_delta)
            h = w * pl.reciprocal(size, approx=True)
            return sums[0] + h * y, sums[1] + h

        empty = (jnp.zeros((chunk, 256), F32), jnp.zeros((chunk, 256), F32))
        top, bottom = lax.fori_loop(0, slots, plain, empty, unroll=4)
        estimate = top / (bottom + prior_weight)
        for _ in range(HUBER_ITERS):
            top, bottom = lax.fori_loop(
                0, slots, functools.partial(robust, estimate), empty, unroll=4
            )
            estimate = top / (bottom + prior_weight / huber_delta)
        field_ref[here, :] = estimate
        return carry

    lax.fori_loop(0, 64 // chunk, merge_rows, 0)
    exact = lax.Precision.HIGHEST
    ordered = jnp.dot(u_ref[...], field_ref[...], precision=exact, preferred_element_type=F32)
    for pair in range(2):
        here = slice(pair * 128, pair * 128 + 128)
        field_ref[:, here] = jnp.dot(
            ordered[:, here], v_ref[...], precision=exact, preferred_element_type=F32
        )


def order_matrices():
    q = np.zeros((128, 256), np.float32)
    u = np.zeros((64, 64), np.float32)
    v = np.zeros((128, 128), np.float32)
    for n in range(64):
        place = (n % 2) * 32 + n // 2
        q[n, place] = 1
        q[64 + n, 128 + place] = 1
        u[n, place] = 1
        v[place, n] = 1
        v[64 + place, 64 + n] = 1
    return jnp.asarray(q, BF), jnp.asarray(u), jnp.asarray(v)


MESH = pl.DeviceIdType.MESH


def exchange_kernel(
    quarters_ref,
    laid_ref,
    sent_ref,
    meta_ref,
    valid_ref,
    order_ref,
    w_in_raw,
    w_hid_raw,
    w_out_raw,
    q_ref,
    u_ref,
    v_ref,
    out_ref,
    planes_ref,
    codes_ref,
    weights_ref,
    matrices_ref,
    x_ref,
    own_ref,
    w_in_ref,
    w_hid_ref,
    stage_even,
    stage_odd,
    stage_code,
    y_ref,
    wt_ref,
    field_ref,
    near_left,
    near_right,
    last_ref,
    local_sems,
    x_send,
    x_recv,
    right_send,
    left_send,
    plane_recv,
    mat_send,
    mat_recv,
    code_send,
    code_recv,
    weight_send,
    weight_recv,
    mat_band_send,
    mat_band_recv,
    weight_band_send,
    weight_band_recv,
    twin_send,
    twin_recv,
    halo_send,
    halo_recv,
):
    tiles = planes_ref.shape[0]
    bands = x_ref.shape[0]
    scenes = laid_ref.shape[0]
    cap = sent_ref.shape[0] // tiles
    tile = lax.axis_index("tile")
    band = lax.axis_index("band")

    def tile_peer(k):
        return lax.rem(tile + k, tiles)

    def tile_source(k):
        return lax.rem(tile + tiles - k, tiles)

    def band_peer(k):
        return lax.rem(band + k, bands)

    def for_tiles(first, body):
        def step(k, carry):
            body(k)
            return carry

        lax.fori_loop(first, tiles, step, 0)

    edge = (tile == 0) | (tile == tiles - 1)
    inner = jnp.minimum(tile, tiles - 1 - tile)
    outward = jnp.where(tile < tiles - 1 - tile, 1, -1)

    def nearest(n):
        near = ((n + 1) // 2) * (1 - 2 * lax.rem(n, 2))
        return tile + jnp.where(n <= 2 * inner, near, (n - inner) * outward)

    barrier = pltpu.get_barrier_semaphore()
    for_tiles(
        1,
        lambda k: pl.semaphore_signal(
            barrier, inc=1, device_id={"tile": tile_peer(k)}, device_id_type=MESH
        ),
    )
    for k in range(1, bands):
        pl.semaphore_signal(barrier, inc=1, device_id={"band": band_peer(k)}, device_id_type=MESH)
    pl.semaphore_wait(barrier, tiles - 1 + bands - 1)

    def remote(src, dst, send, recv, where):
        return pltpu.make_async_remote_copy(
            src_ref=src,
            dst_ref=dst,
            send_sem=send,
            recv_sem=recv,
            device_id=where,
            device_id_type=MESH,
        )

    def x_copy(peer, source):
        return remote(
            quarters_ref.at[peer], x_ref.at[source], x_send.at[peer], x_recv.at[source],
            {"band": peer},
        )

    def plane_copy(shard, target, sems):
        return remote(
            planes_ref.at[shard], planes_ref.at[shard], sems.at[shard], plane_recv.at[shard],
            {"tile": target},
        )

    def own_plane_copy(target, sems):
        return remote(
            laid_ref, planes_ref.at[tile], sems.at[tile], plane_recv.at[tile], {"tile": target}
        )

    def mat_copy(peer, source):
        return remote(
            sent_ref.at[pl.ds(peer * cap, cap)], matrices_ref.at[band, source],
            mat_send.at[peer], mat_recv.at[source], {"tile": peer},
        )

    def code_copy(peer, source):
        return remote(
            meta_ref.at[peer], codes_ref.at[source], code_send.at[peer], code_recv.at[source],
            {"tile": peer},
        )

    parity = lax.rem(tile, 2)
    twin = tile + 1 - 2 * parity

    def weight_copy(peer, source):
        return remote(
            own_ref, weights_ref.at[band, parity, source // 2], weight_send.at[peer],
            weight_recv.at[source], {"tile": peer},
        )

    def mat_band_copy(source, peer, owner):
        return remote(
            matrices_ref.at[owner, source], matrices_ref.at[owner, source],
            mat_band_send.at[peer], mat_band_recv.at[owner], {"band": peer},
        )

    def weight_band_copy(source, peer, owner):
        shard = weights_ref.at[owner, parity, source // 2]
        return remote(
            shard, shard, weight_band_send.at[peer], weight_band_recv.at[owner], {"band": peer}
        )

    def twin_copy(owner, side):
        shard = weights_ref.at[owner, side]
        return remote(shard, shard, twin_send.at[owner], twin_recv.at[owner], {"tile": twin})

    for k in range(1, bands):
        x_copy(band_peer(k), band).start()
    x_local = pltpu.make_async_copy(quarters_ref.at[band], x_ref.at[band], local_sems.at[0])
    x_local.start()

    @pl.when(tile < tiles - 1)
    def _():
        own_plane_copy(tile + 1, right_send).start()

    @pl.when(tile > 0)
    def _():
        own_plane_copy(tile - 1, left_send).start()

    def first_sends(k):
        mat_copy(tile_peer(k), tile).start()
        code_copy(tile_peer(k), tile).start()

    for_tiles(1, first_sends)
    plane_local = pltpu.make_async_copy(laid_ref, planes_ref.at[tile], local_sems.at[1])
    plane_local.start()
    mat_local = pltpu.make_async_copy(
        sent_ref.at[pl.ds(tile * cap, cap)], matrices_ref.at[band, tile], local_sems.at[2]
    )
    mat_local.start()
    code_local = pltpu.make_async_copy(meta_ref.at[tile], codes_ref.at[tile], local_sems.at[3])
    code_local.start()

    def forward(s):
        left, right = tile - s, tile + s

        @pl.when((left >= 0) & (tile < tiles - 1))
        def _():
            plane_copy(left, tile, right_send).wait_recv()
            plane_copy(left, tile + 1, right_send).start()

        @pl.when((right < tiles) & (tile > 0))
        def _():
            plane_copy(right, tile, left_send).wait_recv()
            plane_copy(right, tile - 1, left_send).start()

    def network(scene, carry):
        def silu(t):
            return (t + t * jnp.tanh(t)).astype(BF)

        x = jnp.concatenate([x_ref[b, scene] for b in range(bands)], axis=0)
        hidden = silu(jnp.dot(w_in_ref[...], x, preferred_element_type=F32))
        for layer in range(w_hid_ref.shape[0]):
            hidden = silu(jnp.dot(w_hid_ref[layer], hidden, preferred_element_type=F32))
        w_out = jnp.broadcast_to(w_out_raw[...].astype(F32), (16, w_out_raw.shape[1]))
        logits = jnp.dot(w_out.astype(BF), hidden, preferred_element_type=F32)
        row = jax.nn.sigmoid(-logits[0:1])
        pieces = [row[:, i * 128 : (i + 1) * 128] for i in range(row.shape[1] // 128)]
        shape = (len(pieces), 128)
        line = lax.broadcasted_iota(jnp.int32, shape, 0)
        lane = lax.broadcasted_iota(jnp.int32, shape, 1)
        valid = jnp.zeros(shape, F32)
        side = 2 * len(pieces)
        for i in range(side):
            here = (line == i // 2) & (lane // 64 == i % 2)
            valid = jnp.where(here, valid_ref[scene, band * side + i].astype(F32), valid)
        order = jnp.full(shape, order_ref[scene], jnp.int32).astype(F32)
        recency = jnp.exp(1.4 * order / (scenes * tiles) - 0.7)
        own_ref[scene] = (jnp.concatenate(pieces, axis=0) * valid * recency).astype(BF)
        return carry

    def share_matrices(first, last):
        def share(n, carry):
            source = nearest(n)
            mat_copy(tile, source).wait_recv()
            for j in range(1, bands):
                mat_band_copy(source, band_peer(j), band).start()
            return carry

        lax.fori_loop(first, last, share, 0)

    w_in_ref[...] = (w_in_raw[...].astype(F32) * 0.5).T.astype(BF)
    for layer in range(w_hid_raw.shape[0]):
        w_hid_ref[layer] = (w_hid_raw[layer].astype(F32) * 0.5).T.astype(BF)
    for k in range(1, bands):
        source = lax.rem(band + bands - k, bands)
        x_copy(source, source).wait_recv()
    x_local.wait()
    steps = 1
    for part in range(4):
        if steps < min(4, tiles):
            forward(steps)
            steps += 1
        if part == 2:
            mat_local.wait()
            for k in range(1, bands):
                mat_band_copy(tile, band_peer(k), band).start()
            share_matrices(1, tiles // 2)
        lax.fori_loop(part * scenes // 4, (part + 1) * scenes // 4, network, 0)

    weight_local = pltpu.make_async_copy(
        own_ref, weights_ref.at[band, parity, tile // 2], local_sems.at[4]
    )
    weight_local.start()

    def for_same(body):
        def step(k, carry):
            body(2 * k)
            return carry

        lax.fori_loop(1, tiles // 2, step, 0)

    for_same(lambda k: weight_copy(tile_peer(k), tile).start())
    weight_local.wait()
    for k in range(1, bands):
        weight_band_copy(tile, band_peer(k), band).start()

    def share_weights(n):
        source = nearest(n)

        @pl.when(lax.rem(source + tile, 2) == 0)
        def _():
            weight_copy(tile, source).wait_recv()
            for j in range(1, bands):
                weight_band_copy(source, band_peer(j), band).start()

    share_matrices(tiles // 2, tiles)
    for_tiles(1, share_weights)
    twin_copy(band, parity).start()
    if steps < tiles:
        forward(steps)
        steps += 1
    plane_local.wait()
    code_local.wait()
    for_tiles(1, lambda k: code_copy(tile, tile_source(k)).wait_recv())
    code_copies = pltpu.make_async_copy(codes_ref, stage_code, local_sems.at[4])
    code_copies.start()

    def mat_band_all(peer):
        whole = matrices_ref.at[peer]
        return remote(
            whole, whole, mat_band_send.at[peer], mat_band_recv.at[peer], {"band": peer}
        )

    def weight_band_all(peer, side):
        whole = weights_ref.at[peer, side]
        return remote(
            whole, whole, weight_band_send.at[peer], weight_band_recv.at[peer], {"band": peer}
        )

    for k in range(1, bands):
        peer = band_peer(bands - k)
        mat_band_all(peer).wait_recv()
        weight_band_all(peer, parity).wait_recv()
        twin_copy(peer, parity).start()
    for b in range(bands):
        twin_copy(b, 1 - parity).wait_recv()
    code_copies.wait()

    stages = (stage_even, stage_odd)

    def stage(n, odd):
        return pltpu.make_async_copy(
            planes_ref.at[nearest(n)], stages[odd], local_sems.at[5 + odd]
        )

    stage(0, 0).start()

    def reproject(first, last):
        def turn(m, carry):
            for odd in range(2):
                n = 2 * m + odd
                stage(n, odd).wait()

                @pl.when((n + 1 < tiles) & jnp.logical_not(edge))
                def _():
                    stage(n + 1, 1 - odd).start()

                for r in range(cap):
                    reproject_slot(
                        r, cap, nearest(n), stage_code, stages[odd], weights_ref, matrices_ref,
                        q_ref, y_ref, wt_ref,
                    )

                @pl.when((n + 1 < tiles) & edge)
                def _():
                    plane_copy(nearest(n + 1), tile, right_send).wait_recv()
                    stage(n + 1, 1 - odd).start()

            return carry

        lax.fori_loop(first, last, turn, 0)

    if tiles <= 8:
        reproject(0, tiles // 4)
        for_tiles(steps, forward)
        reproject(tiles // 4, tiles // 2)
    else:
        for_tiles(steps, forward)
        reproject(0, tiles // 2)

    robust_merge(y_ref, wt_ref, field_ref, u_ref, v_ref)

    def halo(target, landing, way):
        return remote(
            field_ref, landing, halo_send.at[way], halo_recv.at[way], {"tile": target}
        )

    @pl.when(tile < tiles - 1)
    def _():
        halo(tile + 1, near_left, 0).start()

    @pl.when(tile > 0)
    def _():
        halo(tile - 1, near_right, 1).start()

    @pl.when(tile == 0)
    def _():
        near_left[...] = jnp.zeros_like(near_left)

    @pl.when(tile == tiles - 1)
    def _():
        near_right[...] = jnp.zeros_like(near_right)

    @pl.when(tile > 0)
    def _():
        halo(tile, near_left, 0).wait_recv()

    @pl.when(tile < tiles - 1)
    def _():
        halo(tile, near_right, 1).wait_recv()

    lane = lax.broadcasted_iota(jnp.int32, (64, 128), 1)
    line = lax.broadcasted_iota(jnp.int32, (64, 128), 0)
    shut = ((lane == 127) & (tile == 0)) | ((lane == 63) & (tile == tiles - 1))
    for c in range(out_ref.shape[0]):
        pair = pl.ds((c // 2) * 128, 128)
        own, low, high = field_ref[:, pair], near_left[:, pair], near_right[:, pair]
        if c % 2 == 0:
            low, high = pltpu.roll(low, 64, 1), pltpu.roll(high, 64, 1)
        else:
            own = pltpu.roll(own, 64, 1)
        g = jnp.where(lane < 64, own, jnp.where(lane < 96, high, low))
        for _ in range(SMOOTH):
            across = pltpu.roll(g, 127, 1) - g
            side = jnp.where(shut, 0.0, across / (1.0 + across * across))
            down = pltpu.roll(g, 63, 0) - g
            upright = jnp.where(line == 63, 0.0, down / (1.0 + down * down))
            g = g + smooth_rate * (
                side - pltpu.roll(side, 1, 1) + (upright - pltpu.roll(upright, 1, 0))
            )
        last_ref[c] = g
        even = last_ref[c, pl.ds(0, 32, stride=2), :]
        odd = last_ref[c, pl.ds(1, 32, stride=2), :]
        out_ref[c] = jnp.where(lane[:32] < 64, even, pltpu.roll(odd, 64, 1))

    @pl.when(tile < tiles - 1)
    def _():
        halo(tile + 1, near_left, 0).wait_send()

    @pl.when(tile > 0)
    def _():
        halo(tile - 1, near_right, 1).wait_send()

    def finish(k):
        code_copy(tile_peer(k), tile).wait_send()
        mat_copy(tile_peer(k), tile).wait_send()

    for_tiles(1, finish)
    for_same(lambda k: weight_copy(tile_peer(k), tile).wait_send())

    def finish_planes(shard):
        @pl.when((shard <= tile) & (tile < tiles - 1))
        def _():
            plane_copy(shard, tile, right_send).wait_send()

        @pl.when((shard >= tile) & (tile > 0))
        def _():
            plane_copy(shard, tile, left_send).wait_send()

    for_tiles(0, finish_planes)
    for k in range(1, bands):
        peer = band_peer(k)
        x_copy(peer, band).wait_send()
        mat_band_all(peer).wait_send()
        weight_band_all(peer, parity).wait_send()
    for b in range(bands):
        twin_copy(b, parity).wait_send()


def exchange(quarters, laid, sent, meta, valid_rows, scene_order, w_in, w_hidden, w_out):
    bands, scenes, part, width = quarters.shape
    tiles = meta.shape[0]
    cap = sent.shape[0] // tiles
    hid = w_in.shape[1]
    layers = w_hidden.shape[0]
    lines = width // 128
    anywhere = pl.BlockSpec(memory_space=pl.ANY)
    vmem = pl.BlockSpec(memory_space=pltpu.VMEM)
    smem = pl.BlockSpec(memory_space=pltpu.SMEM)
    dma = pltpu.SemaphoreType.DMA
    return pl.pallas_call(
        exchange_kernel,
        in_specs=[anywhere] * 4 + [smem] * 2 + [vmem] * 6,
        out_specs=[vmem] + [anywhere] * 2,
        out_shape=[
            jax.ShapeDtypeStruct(laid.shape[1:], F32),
            jax.ShapeDtypeStruct((tiles,) + laid.shape, BF),
            jax.ShapeDtypeStruct(meta.shape, jnp.int32),
        ],
        scratch_shapes=[
            pltpu.VMEM((bands, 2, tiles // 2, scenes, lines, 128), BF),
            pltpu.VMEM((bands, tiles, cap) + sent.shape[1:], BF),
            pltpu.VMEM((bands, scenes, part, width), BF),
            pltpu.VMEM((scenes, lines, 128), BF),
            pltpu.VMEM((hid, bands * part), BF),
            pltpu.VMEM((layers, hid, hid), BF),
            pltpu.VMEM(laid.shape, BF),
            pltpu.VMEM(laid.shape, BF),
            pltpu.SMEM(meta.shape, jnp.int32),
            pltpu.VMEM((tiles * cap, 64, 256), F32),
            pltpu.VMEM((tiles * cap, 64, 128), F32),
            pltpu.VMEM((64, 256), F32),
            pltpu.VMEM((64, 256), F32),
            pltpu.VMEM((64, 256), F32),
            pltpu.VMEM((part, 64, 128), F32),
            dma((7,)),
            dma((bands,)),
            dma((bands,)),
        ]
        + [dma((tiles,))] * 9
        + [dma((bands,))] * 6
        + [dma((2,))] * 2,
        compiler_params=pltpu.CompilerParams(
            collective_id=0, has_side_effects=True, vmem_limit_bytes=40 * 1024 * 1024
        ),
    )(
        quarters, laid, sent, meta, valid_rows, scene_order, w_in, w_hidden, w_out[None, :],
        *order_matrices(),
    )[0]


def per_device(
    granules,
    valid_rows,
    scene_order,
    intersections,
    row_resample,
    col_resample,
    w_in,
    w_hidden,
    w_out,
):
    scenes, group_bands, pixel_count = granules.shape
    top = intersections.shape[1]
    tile_count = lax.axis_size("tile")
    band_count = lax.axis_size("band")
    band = lax.axis_index("band")
    tile = lax.axis_index("tile")
    entry_count = scenes * top
    cap = (entry_count + tile_count - 1) // tile_count + 1
    part = pixel_count // band_count

    laid = granules.reshape(scenes, group_bands, pixel_count // 128, 128)
    quarters = jnp.stack([granules[:, :, b * part : (b + 1) * part] for b in range(band_count)])

    flat_dest = intersections.reshape(entry_count)
    is_dest = flat_dest[None, :] == jnp.arange(tile_count, dtype=jnp.int32)[:, None]
    rank = jnp.cumsum(is_dest.astype(jnp.int32), 1) - 1
    pick = is_dest[:, None, :] & (rank[:, None, :] == jnp.arange(cap)[None, :, None])
    scene_ids = (jnp.arange(entry_count, dtype=jnp.int32) // top + 1)[None, None, :]
    code = jnp.sum(jnp.where(pick, scene_ids, 0), 2) - 1
    meta = jnp.zeros((tile_count, 8, 128), jnp.int32).at[:, 0, :cap].set(code)
    pick = pick.reshape(tile_count * cap, entry_count).astype(BF)
    both = jnp.concatenate(
        [
            lax.dynamic_slice_in_dim(m, band * part, part, 2).reshape(entry_count, part)
            for m in (row_resample, col_resample)
        ],
        1,
    )
    sent = jnp.dot(pick, both, preferred_element_type=F32).astype(BF)
    sent = sent.reshape(tile_count * cap, 2 * part // 128, 128)
    field = exchange(
        quarters, laid, sent, meta, valid_rows, scene_order, w_in, w_hidden, w_out
    )
    return field.reshape(group_bands, pixel_count)


def solution(mesh):
    return jax.shard_map(
        per_device,
        mesh=mesh,
        in_specs=(
            P("tile", "band", None),
            P("tile", None),
            P("tile"),
            P("tile", None),
            P("tile", None, None),
            P("tile", None, None),
            P(),
            P(),
            P(),
        ),
        out_specs=P("band", "tile"),
        check_vma=False,
    )
```
